32 devices in a mesh: blk: 4 (over y, x), grp: 8 (over z, core).
Axes of the slice: x: 2, y: 2, z: 4, core: 2. Of those that a mesh axis runs over, the one named last changes fastest.
Arguments:
- field: float32 [128, 192, 512], P('grp', 'blk'), may hold values from -7 to 7
- x_panel: float32 [192, 144], P('blk'), as said below
- y_factor: float32 [128, 128], replicated, as said below
- z_factor: float32 [512, 512], replicated, as said below
- scaling: float32 [128, 192, 512], P('grp', 'blk'), may hold values from 0.3 to 3
Outputs:
- updated: float32 [128, 192, 512], P('grp', 'blk')
The draws below stay inside these ranges and needn't reach their ends.
Inputs may be any that keep to these rules, and one draw needn't show every extreme that they name: x_panel[x, j] is zero where j - 48 - (x mod 48) lies outside -48 to 48. y_factor[i, k] is zero where the periodic distance of i and k exceeds 48. z_factor[i, k] is zero where the periodic distance of i and k exceeds 48.
All inputs are finite; a program needn't handle non-finite values.
Results may differ from the reference program's by a relative error of at most 0.0003.
Values sent between devices are 32-bit elements; how exact they have to be, the bound alone decides.
A program may use at most 64 MiB of HBM per device.

```python
import math
import jax
import jax.numpy as jnp
from jax import lax

HOR = 48
CX = 48
NZ = 512
NX = 192
NY = 128
N_BLK = 4


def band_values(key, dist, horizon):
    rough = jax.random.uniform(key, dist.shape, jnp.float32, 0.5, 1.5)
    distf = dist.astype(jnp.float32)
    sigma = horizon * 1.0
    weight = 0.8 / (1.4936 * sigma) * jnp.exp(-(distf / sigma) ** 2) * rough
    centre = 1.0 + 0.4 * (rough - 1.0)
    values = jnp.where(dist == 0, centre, weight)
    return jnp.where(jnp.abs(dist) <= horizon, values, 0.0).astype(jnp.float32)


def periodic_band(key, count):
    rowid = jnp.arange(count, dtype=jnp.int32)[:, None]
    colid = jnp.arange(count, dtype=jnp.int32)[None, :]
    dist = (colid - rowid + count // 2) % count - count // 2
    return band_values(key, dist, HOR)


def draw_x_panel(key, part):
    rowid = (jnp.arange(NX, dtype=jnp.int32) % CX)[:, None]
    colid = jnp.arange(CX + 2 * HOR, dtype=jnp.int32)[None, :]
    dist = colid - HOR - rowid
    return band_values(key, dist, HOR)


def draw_y_factor(key, part):
    return periodic_band(key, NY)


def draw_z_factor(key, part):
    return periodic_band(key, NZ)


def wavenumbers(key, count, mode_count):
    lowest = max(1, count // (4 * HOR))
    highest = max(lowest + 1, count // HOR + 1)
    magnitude = jax.random.randint(key, (mode_count,), lowest, highest, dtype=jnp.int32)
    signs = 2 * jax.random.randint(jax.random.fold_in(key, 1), (mode_count,), 0, 2, dtype=jnp.int32) - 1
    return magnitude * signs


def draw_field(key, part):
    subkeys = jax.random.split(jax.random.fold_in(key, 11), 6)
    mode_count = 6
    rows_y = jnp.arange(NY, dtype=jnp.int32)[:, None, None]
    rows_x = jnp.arange(NX, dtype=jnp.int32)[None, :, None]
    rows_z = jnp.arange(NZ, dtype=jnp.int32)[None, None, :]
    wave_y = wavenumbers(subkeys[0], NY, mode_count)
    wave_x = wavenumbers(subkeys[1], NX, mode_count)
    wave_z = wavenumbers(subkeys[2], NZ, mode_count)
    amplitude = jax.random.uniform(subkeys[3], (mode_count,), jnp.float32, 0.5, 1.0)
    phases = jax.random.uniform(subkeys[4], (mode_count,), jnp.float32, 0.0, 6.2831853)
    smooth = jnp.zeros((NY, NX, NZ), jnp.float32)
    for mode_index in range(mode_count):
        frac_y = (wave_y[mode_index] * rows_y % NY).astype(jnp.float32) / NY
        frac_x = (wave_x[mode_index] * rows_x % NX).astype(jnp.float32) / NX
        frac_z = (wave_z[mode_index] * rows_z % NZ).astype(jnp.float32) / NZ
        smooth = smooth + amplitude[mode_index] * jnp.cos(6.2831853 * (frac_y + frac_x + frac_z) + phases[mode_index])
    rough_part = jax.random.truncated_normal(subkeys[5], -4.0, 4.0, (NY, NX, NZ), jnp.float32)
    return (rough_part + 0.3 * smooth).astype(jnp.float32)


def shard_levels(rng, dims, shards, least, top_value):
    level = 1.0
    for axis_at, blocks in shards:
        draws = jax.random.uniform(jax.random.fold_in(jax.random.fold_in(rng, 6), axis_at), (blocks,), jnp.float32, least / len(shards), top_value / len(shards))
        level = level * jnp.repeat(jnp.exp(draws), dims[axis_at] // blocks).reshape((-1,) + (1,) * (len(dims) - 1 - axis_at))
    return level


def setup_inputs(seed: int = 0) -> dict:
    streams_of = jax.random.split(jax.random.key(seed), 6)
    field = draw_field(jax.random.fold_in(streams_of[5], 71), 0)
    x_panel = draw_x_panel(jax.random.fold_in(streams_of[5], 71), 0)
    y_factor = draw_y_factor(jax.random.fold_in(streams_of[5], 71), 0)
    z_factor = draw_z_factor(jax.random.fold_in(streams_of[5], 71), 0)
    scaling = jnp.clip(jnp.exp(math.log(3.0) - 2.3025851 * jax.random.uniform(streams_of[4], (NY, NX, NZ), jnp.float32) ** shard_levels(streams_of[4], (NY, NX, NZ), ((0, 8), (1, 4)), -0.2, 0.2)), 0.3, 3.0)
    return dict(field=field, x_panel=x_panel, y_factor=y_factor, z_factor=z_factor, scaling=scaling)


def apply_depth(block, z_factor):
    return lax.dot_general(block, z_factor, (((2,), (1,)), ((), ())), precision=lax.Precision.HIGHEST)


def reference(field, x_panel, y_factor, z_factor, scaling):
    depth = apply_depth(field, z_factor)
    across = jnp.einsum("yk,kxz->yxz", y_factor, depth, precision=lax.Precision.HIGHEST)
    padded = jnp.concatenate([across[:, NX - HOR:], across, across[:, :HOR]], axis=1)

    def one_block(index):
        start = (index * CX).astype(jnp.int32)
        window = lax.dynamic_slice_in_dim(padded, start, CX + 2 * HOR, 1)
        rows = lax.dynamic_slice_in_dim(x_panel, start, CX, 0)
        return jnp.einsum("rj,yjz->yrz", rows, window, precision=lax.Precision.HIGHEST)

    blocks = lax.map(one_block, jnp.arange(N_BLK, dtype=jnp.int32))
    along = jnp.transpose(blocks, (1, 0, 2, 3)).reshape(NY, NX, NZ)
    return along * scaling
```

```python
import functools

import jax
import jax.numpy as jnp
from jax import lax
from jax.experimental import pallas as pl
from jax.experimental.pallas import tpu as pltpu
from jax.sharding import PartitionSpec as P

LANES = 128
SUB = 16
MESH = pl.DeviceIdType.MESH
F32 = jnp.float32
BF16 = jnp.bfloat16


def padded(cells, sides, width):
    for axis, dim in sides:
        count = lax.axis_size(axis)
        head = lax.slice_in_dim(cells, 0, width, axis=dim)
        tail = lax.slice_in_dim(cells, cells.shape[dim] - width, cells.shape[dim], axis=dim)
        cells = jnp.concatenate(
            [
                lax.ppermute(tail, axis, [(i, (i + 1) % count) for i in range(count)]),
                cells,
                lax.ppermute(head, axis, [((i + 1) % count, i) for i in range(count)]),
            ],
            axis=dim,
        )
    return cells


def apply_depth(block, z_factor):
    return lax.dot_general(
        block, z_factor, (((2,), (1,)), ((), ())), precision=lax.Precision.HIGHEST
    )


def apply_planes(x_panel, widened):
    return jnp.einsum("rj,yjz->yrz", x_panel, widened, precision=lax.Precision.HIGHEST)


def apply_across(block, y_factor):
    rows_here, planes, cells = block.shape
    flat = block.reshape(rows_here, planes * cells)
    pencils = lax.all_to_all(flat, "grp", split_axis=1, concat_axis=0, tiled=True)
    turned = jnp.dot(y_factor, pencils, precision=lax.Precision.HIGHEST)
    back = lax.all_to_all(turned, "grp", split_axis=0, concat_axis=1, tiled=True)
    return back.reshape(rows_here, planes, cells)


def plain(field, x_panel, y_factor, z_factor, scaling):
    width = (x_panel.shape[1] - field.shape[1]) // 2
    widened = padded(field, (("blk", 1),), width)
    planes_done = apply_planes(x_panel, widened)
    depth = apply_depth(planes_done, z_factor)
    along = apply_across(depth, y_factor)
    return along * scaling


def split(value):
    high = value.astype(BF16)
    return high, (value - high.astype(F32)).astype(BF16)


def stacked(value):
    high, low = split(value)
    return jnp.concatenate([high, low], axis=0), high


def times(both, high, right):
    right_high, right_low = split(right)
    rows = high.shape[0]
    first = jnp.dot(both, right_high, preferred_element_type=F32)
    second = jnp.dot(high, right_low, preferred_element_type=F32)
    return first[:rows] + (first[rows:] + second)


def kernel(
    n_grp, n_blk, field, panel, y_factor, z_factor, scaling, out,
    field_high, field_low, own, partner, other, turned, gathered, mixed, back,
    f_send, f_recv, b_send, b_recv, h1_send, h1_recv, h2_send, h2_recv,
):
    rows, planes, cells = field.shape
    chunks = cells // LANES
    share = planes // n_grp
    piece = share * rows
    parts = h1_send.shape[1]
    part_rows = rows // parts
    grp = lax.axis_index("grp")
    blk = lax.axis_index("blk")
    even = lax.rem(blk, 2) == 0
    mate = jnp.where(even, blk + 1, blk - 1)
    ahead = lax.rem(jnp.where(even, blk + 2, blk + n_blk - 2), n_blk)
    behind = lax.rem(jnp.where(even, blk + n_blk - 2, blk + 2), n_blk)

    offsets = sorted(range(1, n_grp), key=lambda s: (-min(s, n_grp - s), s))
    barrier = pltpu.get_barrier_semaphore()
    for step in offsets:
        pl.semaphore_signal(
            barrier, inc=1, device_id={"grp": lax.rem(grp + step, n_grp)}, device_id_type=MESH
        )
    pl.semaphore_signal(barrier, inc=1, device_id={"blk": mate}, device_id_type=MESH)
    pl.semaphore_signal(barrier, inc=1, device_id={"blk": behind}, device_id_type=MESH)

    def depth(chunk):
        z_both, z_high = stacked(z_factor[chunk * LANES:(chunk + 1) * LANES, :])
        turn = (((1,), (1,)), ((), ()))
        for y in range(0, rows, part_rows // 2):
            y_end = y + part_rows // 2
            here = slice(y * planes, y_end * planes)
            first = lax.dot_general(field_high[here, :], z_both, turn, preferred_element_type=F32)
            second = lax.dot_general(field_low[here, :], z_high, turn, preferred_element_type=F32)
            result = first[:, :LANES] + (first[:, LANES:] + second)
            own[chunk, y:y_end] = result.reshape(y_end - y, planes, LANES)

    def rows_of(y):
        return pl.ds(y, planes, stride=rows)

    def scatter(chunk):
        for step in offsets:
            to = lax.rem(grp + step, n_grp)
            pltpu.make_async_remote_copy(
                src_ref=turned.at[chunk, pl.ds(pl.multiple_of(to * piece, SUB), piece)],
                dst_ref=gathered.at[chunk, grp],
                send_sem=f_send.at[chunk],
                recv_sem=f_recv.at[chunk],
                device_id={"grp": to},
                device_id_type=MESH,
            ).start()
        gathered[chunk, grp] = turned[chunk, pl.ds(pl.multiple_of(grp * piece, SUB), piece), :]

    def wait_for(ref, sem):
        pltpu.make_async_copy(ref, ref, sem).wait()

    def across(chunk):
        wait_for(gathered.at[chunk, pl.ds(0, n_grp - 1)], f_recv.at[chunk])
        y_both, y_high = stacked(y_factor[...])
        for at in range(share):
            pencils = jnp.concatenate(
                [gathered[chunk, g, at * rows:(at + 1) * rows, :] for g in range(n_grp)], axis=0
            )
            result = times(y_both, y_high, pencils)
            for g in range(n_grp):
                mixed[chunk, g, at * rows:(at + 1) * rows, :] = result[g * rows:(g + 1) * rows]
        for step in offsets:
            to = lax.rem(grp + step, n_grp)
            pltpu.make_async_remote_copy(
                src_ref=mixed.at[chunk, to],
                dst_ref=back.at[chunk, pl.ds(pl.multiple_of(grp * piece, SUB), piece)],
                send_sem=b_send.at[chunk],
                recv_sem=b_recv.at[chunk],
                device_id={"grp": to},
                device_id_type=MESH,
            ).start()
        back[chunk, pl.ds(pl.multiple_of(grp * piece, SUB), piece), :] = mixed[chunk, grp]

    def wait_back(chunk):
        wait_for(back.at[chunk, pl.ds(0, (n_grp - 1) * piece)], b_recv.at[chunk])

    def part(chunk, at):
        return (chunk, pl.ds(at * part_rows, part_rows))

    def swap(chunk, at):
        return pltpu.make_async_remote_copy(
            src_ref=own.at[part(chunk, at)],
            dst_ref=partner.at[part(chunk, at)],
            send_sem=h1_send.at[chunk, at],
            recv_sem=h1_recv.at[chunk, at],
            device_id={"blk": mate},
            device_id_type=MESH,
        )

    def forward(chunk, at):
        return pltpu.make_async_remote_copy(
            src_ref=partner.at[part(chunk, at)],
            dst_ref=other.at[part(chunk, at)],
            send_sem=h2_send.at[chunk, at],
            recv_sem=h2_recv.at[chunk, at],
            device_id={"blk": ahead},
            device_id_type=MESH,
        )

    def pass_on(chunk):
        for at in range(parts):
            swap(chunk, at).wait_recv()
            forward(chunk, at).start()

    def along(chunk, store):
        left, mid, right = (panel[:, i * planes:(i + 1) * planes] for i in range(3))
        factor = jnp.concatenate(
            [mid, jnp.where(even, right, left), jnp.where(even, left, right)], axis=1
        )
        x_both, x_high = stacked(factor)
        for at in range(parts):
            forward(chunk, at).wait_recv()
            for y in range(at * part_rows, (at + 1) * part_rows, 2):
                wide = jnp.concatenate(
                    [
                        jnp.concatenate([held[chunk, y + k] for held in (own, partner, other)], axis=0)
                        for k in range(2)
                    ],
                    axis=1,
                )
                result = times(x_both, x_high, wide)
                for k in range(2):
                    store(chunk, y + k, result[:, k * LANES:(k + 1) * LANES])

    def store_turned(chunk, y, value):
        turned[chunk, rows_of(y), :] = value

    def store_out(chunk, y, value):
        lanes = slice(chunk * LANES, (chunk + 1) * LANES)
        out[y, :, lanes] = value * scaling[y, :, lanes]

    flat = field[...].reshape(rows * planes, cells)
    field_high[...], field_low[...] = split(flat)
    depth(0)
    for y in range(rows):
        store_turned(0, y, own[0, y])
    pl.semaphore_wait(barrier, len(offsets) + 2)
    scatter(0)
    for chunk in range(1, chunks):
        depth(chunk)
        for at in range(parts):
            swap(chunk, at).start()

    def first_home():
        wait_back(0)
        for y in range(rows):
            own[0, y] = back[0, rows_of(y), :]
        for at in range(parts):
            swap(0, at).start()

    for chunk in range(1, chunks):
        pass_on(chunk)
        if chunk == 1:
            across(0)
        elif chunk == 2:
            first_home()
        else:
            across(chunk - 2)
        along(chunk, store_turned)
        scatter(chunk)
    if chunks < 2:
        across(0)
    if chunks < 3:
        first_home()
    pass_on(0)
    late = range(max(1, chunks - 2), chunks)
    for chunk in late[:-1]:
        across(chunk)
    along(0, store_out)
    for chunk in late[-1:]:
        across(chunk)
    for chunk in range(1, chunks):
        wait_back(chunk)
        for y in range(rows):
            store_out(chunk, y, back[chunk, rows_of(y), :])
    for chunk in range(chunks):
        wait_for(gathered.at[chunk, pl.ds(0, n_grp - 1)], f_send.at[chunk])
        wait_for(gathered.at[chunk, pl.ds(0, n_grp - 1)], b_send.at[chunk])
        for at in range(parts):
            swap(chunk, at).wait_send()
            forward(chunk, at).wait_send()


def fused(field, x_panel, y_factor, z_factor, scaling):
    n_grp, n_blk = lax.axis_size("grp"), lax.axis_size("blk")
    rows, planes, cells = field.shape
    chunks = cells // LANES
    piece = planes // n_grp * rows
    parts = 2
    whole = pl.BlockSpec(memory_space=pltpu.VMEM)
    held = pltpu.VMEM((chunks, rows, planes, LANES), F32)
    turned = pltpu.VMEM((chunks, planes * rows, LANES), F32)
    pieces = pltpu.VMEM((chunks, n_grp, piece, LANES), F32)
    return pl.pallas_call(
        functools.partial(kernel, n_grp, n_blk),
        out_shape=jax.ShapeDtypeStruct(field.shape, F32),
        in_specs=[whole] * 5,
        out_specs=whole,
        scratch_shapes=[pltpu.VMEM((rows * planes, cells), BF16)] * 2
        + [held] * 3
        + [turned, pieces, pieces, turned]
        + [pltpu.SemaphoreType.DMA((chunks,))] * 4
        + [pltpu.SemaphoreType.DMA((chunks, parts))] * 4,
        compiler_params=pltpu.CompilerParams(
            collective_id=0, has_side_effects=True, vmem_limit_bytes=48 * 2**20
        ),
    )(field, x_panel, y_factor, z_factor, scaling)


def on_device(field, x_panel, y_factor, z_factor, scaling):
    n_grp, n_blk = lax.axis_size("grp"), lax.axis_size("blk")
    rows, planes, cells = field.shape
    fits = (
        x_panel.shape[1] == 3 * planes
        and n_blk >= 4
        and n_blk % 2 == 0
        and n_grp >= 2
        and planes % n_grp == 0
        and planes % SUB == 0
        and rows % SUB == 0
        and cells % LANES == 0
    )
    step = fused if fits else plain
    return step(field, x_panel, y_factor, z_factor, scaling)


def solution(mesh):
    in_specs = (P("grp", "blk", None), P("blk", None), P(), P(), P("grp", "blk", None))
    out_specs = P("grp", "blk", None)
    return jax.shard_map(
        on_device, mesh=mesh, in_specs=in_specs, out_specs=out_specs, check_vma=False
    )
```

```python
import functools

import jax
import jax.numpy as jnp
from jax import lax
from jax.experimental import pallas as pl
from jax.experimental.pallas import tpu as pltpu
from jax.sharding import PartitionSpec as P

LANES = 128
SUB = 16
FETCHES = 4
MESH = pl.DeviceIdType.MESH
F32 = jnp.float32
BF16 = jnp.bfloat16


def padded(cells, sides, width):
    for axis, dim in sides:
        count = lax.axis_size(axis)
        head = lax.slice_in_dim(cells, 0, width, axis=dim)
        tail = lax.slice_in_dim(cells, cells.shape[dim] - width, cells.shape[dim], axis=dim)
        cells = jnp.concatenate(
            [
                lax.ppermute(tail, axis, [(i, (i + 1) % count) for i in range(count)]),
                cells,
                lax.ppermute(head, axis, [((i + 1) % count, i) for i in range(count)]),
            ],
            axis=dim,
        )
    return cells


def apply_depth(block, z_factor):
    return lax.dot_general(
        block, z_factor, (((2,), (1,)), ((), ())), precision=lax.Precision.HIGHEST
    )


def apply_planes(x_panel, widened):
    return jnp.einsum("rj,yjz->yrz", x_panel, widened, precision=lax.Precision.HIGHEST)


def apply_across(block, y_factor):
    rows_here, planes, cells = block.shape
    flat = block.reshape(rows_here, planes * cells)
    pencils = lax.all_to_all(flat, "grp", split_axis=1, concat_axis=0, tiled=True)
    turned = jnp.dot(y_factor, pencils, precision=lax.Precision.HIGHEST)
    back = lax.all_to_all(turned, "grp", split_axis=0, concat_axis=1, tiled=True)
    return back.reshape(rows_here, planes, cells)


def plain(field, x_panel, y_factor, z_factor, scaling):
    width = (x_panel.shape[1] - field.shape[1]) // 2
    widened = padded(field, (("blk", 1),), width)
    planes_done = apply_planes(x_panel, widened)
    depth = apply_depth(planes_done, z_factor)
    along = apply_across(depth, y_factor)
    return along * scaling


def split(value):
    high = value.astype(BF16)
    return high, (value - high.astype(F32)).astype(BF16)


def stacked(value):
    high, low = split(value)
    return jnp.concatenate([high, low], axis=0), high


def times(both, high, right):
    right_high, right_low = split(right)
    rows = high.shape[0]
    first = jnp.dot(both, right_high, preferred_element_type=F32)
    second = jnp.dot(high, right_low, preferred_element_type=F32)
    return first[:rows] + (first[rows:] + second)


def kernel(
    n_grp, n_blk, field_in, panel_in, y_in, z_in, scaling_in, out,
    field, panel, y_factor, z_factor, scaling,
    field_high, field_low, own, partner, other, turned, gathered, mixed, back,
    in_sem, f_send, f_recv, b_send, b_recv, h1_send, h1_recv, h2_send, h2_recv,
):
    rows, planes, cells = field.shape
    step_rows = rows // FETCHES
    row_parts = [pl.ds(i * step_rows, step_rows) for i in range(FETCHES)]
    heads = [pl.ds(0, LANES), pl.ds(LANES, cells - LANES)][: 1 + (cells > LANES)]
    sources = [(z_in.at[heads[0]], z_factor.at[heads[0]])]
    sources += [(field_in.at[at], field.at[at]) for at in row_parts]
    sources += [(z_in.at[at], z_factor.at[at]) for at in heads[1:]]
    sources += [(y_in, y_factor), (panel_in, panel), (scaling_in, scaling)]
    fetches = [pltpu.make_async_copy(*pair, in_sem.at[i]) for i, pair in enumerate(sources)]
    for fetch in fetches:
        fetch.start()
    chunks = cells // LANES
    share = planes // n_grp
    piece = share * rows
    parts = h1_send.shape[1]
    part_rows = rows // parts
    subs = f_send.shape[1]
    sub = share // subs
    sub_piece = sub * rows
    grp = lax.axis_index("grp")
    blk = lax.axis_index("blk")
    even = lax.rem(blk, 2) == 0
    mate = jnp.where(even, blk + 1, blk - 1)
    ahead = lax.rem(jnp.where(even, blk + 2, blk + n_blk - 2), n_blk)
    behind = lax.rem(jnp.where(even, blk + n_blk - 2, blk + 2), n_blk)

    offsets = sorted(range(1, n_grp), key=lambda s: (-min(s, n_grp - s), s))
    barrier = pltpu.get_barrier_semaphore()
    for step in offsets:
        pl.semaphore_signal(
            barrier, inc=1, device_id={"grp": lax.rem(grp + step, n_grp)}, device_id_type=MESH
        )
    pl.semaphore_signal(barrier, inc=1, device_id={"blk": mate}, device_id_type=MESH)
    pl.semaphore_signal(barrier, inc=1, device_id={"blk": behind}, device_id_type=MESH)

    def depth(chunk):
        z_both, z_high = stacked(z_factor[chunk * LANES:(chunk + 1) * LANES, :])
        turn = (((1,), (1,)), ((), ()))
        for y in range(0, rows, step_rows):
            y_end = y + step_rows
            here = slice(y * planes, y_end * planes)
            if chunk == 0:
                fetches[1 + y // step_rows].wait()
                flat = field[y:y_end].reshape(step_rows * planes, cells)
                field_high[here, :], field_low[here, :] = split(flat)
            first = lax.dot_general(field_high[here, :], z_both, turn, preferred_element_type=F32)
            second = lax.dot_general(field_low[here, :], z_high, turn, preferred_element_type=F32)
            result = first[:, :LANES] + (first[:, LANES:] + second)
            result = result.reshape(step_rows, planes, LANES)
            if chunk == 0:
                for k in range(step_rows):
                    store_turned(chunk, y + k, result[k])
            else:
                own[chunk, y:y_end] = result

    def rows_of(y):
        return pl.ds(y, planes, stride=rows)

    def spot(device, at):
        return pl.ds(pl.multiple_of(device * piece + at * sub_piece, SUB), sub_piece)

    def scatter(chunk):
        for at in range(subs):
            within = pl.ds(at * sub_piece, sub_piece)
            for step in offsets:
                to = lax.rem(grp + step, n_grp)
                pltpu.make_async_remote_copy(
                    src_ref=turned.at[chunk, spot(to, at)],
                    dst_ref=gathered.at[chunk, grp, within],
                    send_sem=f_send.at[chunk, at],
                    recv_sem=f_recv.at[chunk, at],
                    device_id={"grp": to},
                    device_id_type=MESH,
                ).start()
        mine = pl.ds(pl.multiple_of(grp * piece, SUB), piece)
        gathered[chunk, grp] = turned[chunk, mine, :]

    def wait_for(ref, sem):
        pltpu.make_async_copy(ref, ref, sem).wait()

    def incoming(chunk):
        return gathered.at[chunk, pl.ds(0, n_grp - 1), pl.ds(0, sub_piece)]

    def across(chunk):
        y_both, y_high = stacked(y_factor[...])
        for at in range(subs):
            wait_for(incoming(chunk), f_recv.at[chunk, at])
            for plane in range(at * sub, (at + 1) * sub):
                here = slice(plane * rows, (plane + 1) * rows)
                pencils = jnp.concatenate(
                    [gathered[chunk, g, here, :] for g in range(n_grp)], axis=0
                )
                result = times(y_both, y_high, pencils)
                for g in range(n_grp):
                    mixed[chunk, g, here, :] = result[g * rows:(g + 1) * rows]
            within = pl.ds(at * sub_piece, sub_piece)
            for step in offsets:
                to = lax.rem(grp + step, n_grp)
                pltpu.make_async_remote_copy(
                    src_ref=mixed.at[chunk, to, within],
                    dst_ref=back.at[chunk, spot(grp, at)],
                    send_sem=b_send.at[chunk, at],
                    recv_sem=b_recv.at[chunk, at],
                    device_id={"grp": to},
                    device_id_type=MESH,
                ).start()
            back[chunk, spot(grp, at), :] = mixed[chunk, grp, at * sub_piece:(at + 1) * sub_piece, :]

    def wait_back(chunk):
        for at in range(subs):
            wait_for(back.at[chunk, pl.ds(0, (n_grp - 1) * sub_piece)], b_recv.at[chunk, at])

    def part(chunk, at):
        return (chunk, pl.ds(at * part_rows, part_rows))

    def swap(chunk, at):
        return pltpu.make_async_remote_copy(
            src_ref=own.at[part(chunk, at)],
            dst_ref=partner.at[part(chunk, at)],
            send_sem=h1_send.at[chunk, at],
            recv_sem=h1_recv.at[chunk, at],
            device_id={"blk": mate},
            device_id_type=MESH,
        )

    def forward(chunk, at):
        return pltpu.make_async_remote_copy(
            src_ref=partner.at[part(chunk, at)],
            dst_ref=other.at[part(chunk, at)],
            send_sem=h2_send.at[chunk, at],
            recv_sem=h2_recv.at[chunk, at],
            device_id={"blk": ahead},
            device_id_type=MESH,
        )

    def pass_on(chunk):
        for at in range(parts):
            swap(chunk, at).wait_recv()
            forward(chunk, at).start()

    def along(chunk, store):
        left, mid, right = (panel[:, i * planes:(i + 1) * planes] for i in range(3))
        factor = jnp.concatenate(
            [mid, jnp.where(even, right, left), jnp.where(even, left, right)], axis=1
        )
        x_both, x_high = stacked(factor)
        for at in range(parts):
            forward(chunk, at).wait_recv()
            for y in range(at * part_rows, (at + 1) * part_rows, 2):
                wide = jnp.concatenate(
                    [
                        jnp.concatenate([held[chunk, y + k] for held in (own, partner, other)], axis=0)
                        for k in range(2)
                    ],
                    axis=1,
                )
                result = times(x_both, x_high, wide)
                for k in range(2):
                    store(chunk, y + k, result[:, k * LANES:(k + 1) * LANES])

    def store_turned(chunk, y, value):
        turned[chunk, rows_of(y), :] = value

    def store_out(chunk, y, value):
        lanes = slice(chunk * LANES, (chunk + 1) * LANES)
        out[y, :, lanes] = value * scaling[y, :, lanes]

    fetches[0].wait()
    depth(0)
    pl.semaphore_wait(barrier, len(offsets) + 2)
    scatter(0)
    for fetch in fetches[1 + FETCHES:]:
        fetch.wait()
    for chunk in range(1, chunks):
        depth(chunk)
        for at in range(parts):
            swap(chunk, at).start()

    def first_home():
        wait_back(0)
        for y in range(rows):
            own[0, y] = back[0, rows_of(y), :]
        for at in range(parts):
            swap(0, at).start()

    for chunk in range(1, chunks):
        pass_on(chunk)
        if chunk == 1:
            across(0)
        elif chunk == 2:
            first_home()
        else:
            across(chunk - 2)
        along(chunk, store_turned)
        scatter(chunk)
    if chunks < 2:
        across(0)
    if chunks < 3:
        first_home()
    pass_on(0)
    late = range(max(1, chunks - 2), chunks)
    for chunk in late[:-1]:
        across(chunk)
    along(0, store_out)
    for chunk in late[-1:]:
        across(chunk)
    for chunk in range(1, chunks):
        wait_back(chunk)
        for y in range(rows):
            store_out(chunk, y, back[chunk, rows_of(y), :])
    for chunk in range(chunks):
        for at in range(subs):
            wait_for(incoming(chunk), f_send.at[chunk, at])
            wait_for(incoming(chunk), b_send.at[chunk, at])
        for at in range(parts):
            swap(chunk, at).wait_send()
            forward(chunk, at).wait_send()


def fused(field, x_panel, y_factor, z_factor, scaling):
    n_grp, n_blk = lax.axis_size("grp"), lax.axis_size("blk")
    rows, planes, cells = field.shape
    chunks = cells // LANES
    share = planes // n_grp
    piece = share * rows
    parts = 2
    subs = 2 if share % 2 == 0 else 1
    held = pltpu.VMEM((chunks, rows, planes, LANES), F32)
    turned = pltpu.VMEM((chunks, planes * rows, LANES), F32)
    pieces = pltpu.VMEM((chunks, n_grp, piece, LANES), F32)
    return pl.pallas_call(
        functools.partial(kernel, n_grp, n_blk),
        out_shape=jax.ShapeDtypeStruct(field.shape, F32),
        in_specs=[pl.BlockSpec(memory_space=pltpu.HBM)] * 5,
        out_specs=pl.BlockSpec(memory_space=pltpu.VMEM),
        scratch_shapes=[
            pltpu.VMEM(array.shape, F32) for array in (field, x_panel, y_factor, z_factor, scaling)
        ]
        + [pltpu.VMEM((rows * planes, cells), BF16)] * 2
        + [held] * 3
        + [turned, pieces, pieces, turned]
        + [pltpu.SemaphoreType.DMA((5 + FETCHES,))]
        + [pltpu.SemaphoreType.DMA((chunks, subs))] * 4
        + [pltpu.SemaphoreType.DMA((chunks, parts))] * 4,
        compiler_params=pltpu.CompilerParams(
            collective_id=0, has_side_effects=True, vmem_limit_bytes=48 * 2**20
        ),
    )(field, x_panel, y_factor, z_factor, scaling)


def on_device(field, x_panel, y_factor, z_factor, scaling):
    n_grp, n_blk = lax.axis_size("grp"), lax.axis_size("blk")
    rows, planes, cells = field.shape
    fits = (
        x_panel.shape[1] == 3 * planes
        and n_blk >= 4
        and n_blk % 2 == 0
        and n_grp >= 2
        and planes % n_grp == 0
        and planes % SUB == 0
        and rows % SUB == 0
        and cells % LANES == 0
    )
    step = fused if fits else plain
    return step(field, x_panel, y_factor, z_factor, scaling)


def solution(mesh):
    in_specs = (P("grp", "blk", None), P("blk", None), P(), P(), P("grp", "blk", None))
    out_specs = P("grp", "blk", None)
    return jax.shard_map(
        on_device, mesh=mesh, in_specs=in_specs, out_specs=out_specs, check_vma=False
    )
```

```python
import functools

import jax
import jax.numpy as jnp
from jax import lax
from jax.experimental import pallas as pl
from jax.experimental.pallas import tpu as pltpu
from jax.sharding import PartitionSpec as P

LANES = 128
SUB = 16
FETCHES = 4
MESH = pl.DeviceIdType.MESH
F32 = jnp.float32
BF16 = jnp.bfloat16


def padded(cells, sides, width):
    for axis, dim in sides:
        count = lax.axis_size(axis)
        head = lax.slice_in_dim(cells, 0, width, axis=dim)
        tail = lax.slice_in_dim(cells, cells.shape[dim] - width, cells.shape[dim], axis=dim)
        cells = jnp.concatenate(
            [
                lax.ppermute(tail, axis, [(i, (i + 1) % count) for i in range(count)]),
                cells,
                lax.ppermute(head, axis, [((i + 1) % count, i) for i in range(count)]),
            ],
            axis=dim,
        )
    return cells


def apply_depth(block, z_factor):
    return lax.dot_general(
        block, z_factor, (((2,), (1,)), ((), ())), precision=lax.Precision.HIGHEST
    )


def apply_planes(x_panel, widened):
    return jnp.einsum("rj,yjz->yrz", x_panel, widened, precision=lax.Precision.HIGHEST)


def apply_across(block, y_factor):
    rows_here, planes, cells = block.shape
    flat = block.reshape(rows_here, planes * cells)
    pencils = lax.all_to_all(flat, "grp", split_axis=1, concat_axis=0, tiled=True)
    turned = jnp.dot(y_factor, pencils, precision=lax.Precision.HIGHEST)
    back = lax.all_to_all(turned, "grp", split_axis=0, concat_axis=1, tiled=True)
    return back.reshape(rows_here, planes, cells)


def plain(field, x_panel, y_factor, z_factor, scaling):
    width = (x_panel.shape[1] - field.shape[1]) // 2
    widened = padded(field, (("blk", 1),), width)
    planes_done = apply_planes(x_panel, widened)
    depth = apply_depth(planes_done, z_factor)
    along = apply_across(depth, y_factor)
    return along * scaling


def split(value):
    high = value.astype(BF16)
    return high, (value - high.astype(F32)).astype(BF16)


def stacked(value):
    high, low = split(value)
    return jnp.concatenate([high, low], axis=0), high


def times(both, high, right):
    right_high, right_low = split(right)
    rows = high.shape[0]
    first = jnp.dot(both, right_high, preferred_element_type=F32)
    second = jnp.dot(high, right_low, preferred_element_type=F32)
    return first[:rows] + (first[rows:] + second)


def kernel(
    n_grp, n_blk, field_in, panel_in, y_in, z_in, scaling_in, out,
    field, panel, y_factor, z_factor, scaling, done,
    field_high, field_low, own, partner, other, turned, gathered, mixed, back,
    in_sem, out_sem, f_send, f_recv, b_send, b_recv, h1_send, h1_recv, h2_send, h2_recv,
):
    rows, planes, cells = field.shape
    step_rows = rows // FETCHES
    row_parts = [pl.ds(i * step_rows, step_rows) for i in range(FETCHES)]
    heads = [pl.ds(0, LANES), pl.ds(LANES, cells - LANES)][: 1 + (cells > LANES)]
    sources = [(z_in.at[heads[0]], z_factor.at[heads[0]])]
    sources += [(field_in.at[at], field.at[at]) for at in row_parts]
    sources += [(z_in.at[at], z_factor.at[at]) for at in heads[1:]]
    sources += [(y_in, y_factor), (panel_in, panel), (scaling_in, scaling)]
    fetches = [pltpu.make_async_copy(*pair, in_sem.at[i]) for i, pair in enumerate(sources)]
    for fetch in fetches:
        fetch.start()
    chunks = cells // LANES
    share = planes // n_grp
    piece = share * rows
    parts = h1_send.shape[1]
    part_rows = rows // parts
    subs = f_send.shape[1]
    sub = share // subs
    sub_piece = sub * rows
    grp = lax.axis_index("grp")
    blk = lax.axis_index("blk")
    even = lax.rem(blk, 2) == 0
    mate = jnp.where(even, blk + 1, blk - 1)
    ahead = lax.rem(jnp.where(even, blk + 2, blk + n_blk - 2), n_blk)
    behind = lax.rem(jnp.where(even, blk + n_blk - 2, blk + 2), n_blk)

    offsets = sorted(range(1, n_grp), key=lambda s: (-min(s, n_grp - s), s))
    barrier = pltpu.get_barrier_semaphore()
    for step in offsets:
        pl.semaphore_signal(
            barrier, inc=1, device_id={"grp": lax.rem(grp + step, n_grp)}, device_id_type=MESH
        )
    pl.semaphore_signal(barrier, inc=1, device_id={"blk": mate}, device_id_type=MESH)
    pl.semaphore_signal(barrier, inc=1, device_id={"blk": behind}, device_id_type=MESH)

    def depth(chunk):
        z_both, z_high = stacked(z_factor[chunk * LANES:(chunk + 1) * LANES, :])
        turn = (((1,), (1,)), ((), ()))
        for y in range(0, rows, step_rows):
            y_end = y + step_rows
            here = slice(y * planes, y_end * planes)
            if chunk == 0:
                fetches[1 + y // step_rows].wait()
                flat = field[y:y_end].reshape(step_rows * planes, cells)
                field_high[here, :], field_low[here, :] = split(flat)
            first = lax.dot_general(field_high[here, :], z_both, turn, preferred_element_type=F32)
            second = lax.dot_general(field_low[here, :], z_high, turn, preferred_element_type=F32)
            result = first[:, :LANES] + (first[:, LANES:] + second)
            result = result.reshape(step_rows, planes, LANES)
            if chunk == 0:
                for k in range(step_rows):
                    store_turned(chunk, y + k, result[k])
            else:
                own[chunk, y:y_end] = result

    def rows_of(y):
        return pl.ds(y, planes, stride=rows)

    def spot(device, at):
        return pl.ds(pl.multiple_of(device * piece + at * sub_piece, SUB), sub_piece)

    def scatter(chunk):
        for at in range(subs):
            within = pl.ds(at * sub_piece, sub_piece)
            for step in offsets:
                to = lax.rem(grp + step, n_grp)
                pltpu.make_async_remote_copy(
                    src_ref=turned.at[chunk, spot(to, at)],
                    dst_ref=gathered.at[chunk, grp, within],
                    send_sem=f_send.at[chunk, at],
                    recv_sem=f_recv.at[chunk, at],
                    device_id={"grp": to},
                    device_id_type=MESH,
                ).start()
        mine = pl.ds(pl.multiple_of(grp * piece, SUB), piece)
        gathered[chunk, grp] = turned[chunk, mine, :]

    def wait_for(ref, sem):
        pltpu.make_async_copy(ref, ref, sem).wait()

    def incoming(chunk):
        return gathered.at[chunk, pl.ds(0, n_grp - 1), pl.ds(0, sub_piece)]

    def across(chunk):
        y_both, y_high = stacked(y_factor[...])
        for at in range(subs):
            wait_for(incoming(chunk), f_recv.at[chunk, at])
            for plane in range(at * sub, (at + 1) * sub):
                here = slice(plane * rows, (plane + 1) * rows)
                pencils = jnp.concatenate(
                    [gathered[chunk, g, here, :] for g in range(n_grp)], axis=0
                )
                result = times(y_both, y_high, pencils)
                for g in range(n_grp):
                    mixed[chunk, g, here, :] = result[g * rows:(g + 1) * rows]
            within = pl.ds(at * sub_piece, sub_piece)
            for step in offsets:
                to = lax.rem(grp + step, n_grp)
                pltpu.make_async_remote_copy(
                    src_ref=mixed.at[chunk, to, within],
                    dst_ref=back.at[chunk, spot(grp, at)],
                    send_sem=b_send.at[chunk, at],
                    recv_sem=b_recv.at[chunk, at],
                    device_id={"grp": to},
                    device_id_type=MESH,
                ).start()
            back[chunk, spot(grp, at), :] = mixed[chunk, grp, at * sub_piece:(at + 1) * sub_piece, :]

    def wait_back(chunk):
        for at in range(subs):
            wait_for(back.at[chunk, pl.ds(0, (n_grp - 1) * sub_piece)], b_recv.at[chunk, at])

    def part(chunk, at):
        return (chunk, pl.ds(at * part_rows, part_rows))

    def swap(chunk, at):
        return pltpu.make_async_remote_copy(
            src_ref=own.at[part(chunk, at)],
            dst_ref=partner.at[part(chunk, at)],
            send_sem=h1_send.at[chunk, at],
            recv_sem=h1_recv.at[chunk, at],
            device_id={"blk": mate},
            device_id_type=MESH,
        )

    def forward(chunk, at):
        return pltpu.make_async_remote_copy(
            src_ref=partner.at[part(chunk, at)],
            dst_ref=other.at[part(chunk, at)],
            send_sem=h2_send.at[chunk, at],
            recv_sem=h2_recv.at[chunk, at],
            device_id={"blk": ahead},
            device_id_type=MESH,
        )

    def pass_on(chunk):
        for at in range(parts):
            swap(chunk, at).wait_recv()
            forward(chunk, at).start()

    def along(chunk, store):
        left, mid, right = (panel[:, i * planes:(i + 1) * planes] for i in range(3))
        factor = jnp.concatenate(
            [mid, jnp.where(even, right, left), jnp.where(even, left, right)], axis=1
        )
        x_both, x_high = stacked(factor)
        for at in range(parts):
            forward(chunk, at).wait_recv()
            for y in range(at * part_rows, (at + 1) * part_rows, 2):
                wide = jnp.concatenate(
                    [
                        jnp.concatenate([held[chunk, y + k] for held in (own, partner, other)], axis=0)
                        for k in range(2)
                    ],
                    axis=1,
                )
                result = times(x_both, x_high, wide)
                for k in range(2):
                    store(chunk, y + k, result[:, k * LANES:(k + 1) * LANES])

    def store_turned(chunk, y, value):
        turned[chunk, rows_of(y), :] = value

    def written(chunk, at):
        return pltpu.make_async_copy(
            done.at[chunk, row_parts[at]],
            out.at[row_parts[at], :, pl.ds(chunk * LANES, LANES)],
            out_sem.at[chunk, at],
        )

    def store_out(chunk, y, value):
        done[chunk, y] = value * scaling[y, :, chunk * LANES:(chunk + 1) * LANES]
        if (y + 1) % step_rows == 0:
            written(chunk, y // step_rows).start()

    fetches[0].wait()
    depth(0)
    pl.semaphore_wait(barrier, len(offsets) + 2)
    scatter(0)
    for fetch in fetches[1 + FETCHES:]:
        fetch.wait()
    for chunk in range(1, chunks):
        depth(chunk)
        for at in range(parts):
            swap(chunk, at).start()

    def first_home():
        wait_back(0)
        for y in range(rows):
            own[0, y] = back[0, rows_of(y), :]
        for at in range(parts):
            swap(0, at).start()

    for chunk in range(1, chunks):
        pass_on(chunk)
        if chunk == 1:
            across(0)
        elif chunk == 2:
            first_home()
        else:
            across(chunk - 2)
        along(chunk, store_turned)
        scatter(chunk)
    if chunks < 2:
        across(0)
    if chunks < 3:
        first_home()
    pass_on(0)
    late = range(max(1, chunks - 2), chunks)
    for chunk in late[:-1]:
        across(chunk)
    along(0, store_out)
    for chunk in late[-1:]:
        across(chunk)
    for chunk in range(1, chunks):
        wait_back(chunk)
        for y in range(rows):
            store_out(chunk, y, back[chunk, rows_of(y), :])
    for chunk in range(chunks):
        for at in range(FETCHES):
            written(chunk, at).wait()
        for at in range(subs):
            wait_for(incoming(chunk), f_send.at[chunk, at])
            wait_for(incoming(chunk), b_send.at[chunk, at])
        for at in range(parts):
            swap(chunk, at).wait_send()
            forward(chunk, at).wait_send()


def fused(field, x_panel, y_factor, z_factor, scaling):
    n_grp, n_blk = lax.axis_size("grp"), lax.axis_size("blk")
    rows, planes, cells = field.shape
    chunks = cells // LANES
    share = planes // n_grp
    piece = share * rows
    parts = 4
    subs = 2 if share % 2 == 0 else 1
    held = pltpu.VMEM((chunks, rows, planes, LANES), F32)
    turned = pltpu.VMEM((chunks, planes * rows, LANES), F32)
    pieces = pltpu.VMEM((chunks, n_grp, piece, LANES), F32)
    return pl.pallas_call(
        functools.partial(kernel, n_grp, n_blk),
        out_shape=jax.ShapeDtypeStruct(field.shape, F32),
        in_specs=[pl.BlockSpec(memory_space=pltpu.HBM)] * 5,
        out_specs=pl.BlockSpec(memory_space=pltpu.HBM),
        scratch_shapes=[
            pltpu.VMEM(array.shape, F32) for array in (field, x_panel, y_factor, z_factor, scaling)
        ]
        + [held]
        + [pltpu.VMEM((rows * planes, cells), BF16)] * 2
        + [held] * 3
        + [turned, pieces, pieces, turned]
        + [pltpu.SemaphoreType.DMA((5 + FETCHES,))]
        + [pltpu.SemaphoreType.DMA((chunks, FETCHES))]
        + [pltpu.SemaphoreType.DMA((chunks, subs))] * 4
        + [pltpu.SemaphoreType.DMA((chunks, parts))] * 4,
        compiler_params=pltpu.CompilerParams(
            collective_id=0, has_side_effects=True, vmem_limit_bytes=60 * 2**20
        ),
    )(field, x_panel, y_factor, z_factor, scaling)


def on_device(field, x_panel, y_factor, z_factor, scaling):
    n_grp, n_blk = lax.axis_size("grp"), lax.axis_size("blk")
    rows, planes, cells = field.shape
    fits = (
        x_panel.shape[1] == 3 * planes
        and n_blk >= 4
        and n_blk % 2 == 0
        and n_grp >= 2
        and planes % n_grp == 0
        and planes % SUB == 0
        and rows % SUB == 0
        and cells % LANES == 0
    )
    step = fused if fits else plain
    return step(field, x_panel, y_factor, z_factor, scaling)


def solution(mesh):
    in_specs = (P("grp", "blk", None), P("blk", None), P(), P(), P("grp", "blk", None))
    out_specs = P("grp", "blk", None)
    return jax.shard_map(
        on_device, mesh=mesh, in_specs=in_specs, out_specs=out_specs, check_vma=False
    )
```

```python
import functools

import jax
import jax.numpy as jnp
from jax import lax
from jax.experimental import pallas as pl
from jax.experimental.pallas import tpu as pltpu
from jax.sharding import PartitionSpec as P

LANES = 128
SUB = 16
FETCHES = 4
MESH = pl.DeviceIdType.MESH
F32 = jnp.float32
BF16 = jnp.bfloat16


def padded(cells, sides, width):
    for axis, dim in sides:
        count = lax.axis_size(axis)
        head = lax.slice_in_dim(cells, 0, width, axis=dim)
        tail = lax.slice_in_dim(cells, cells.shape[dim] - width, cells.shape[dim], axis=dim)
        cells = jnp.concatenate(
            [
                lax.ppermute(tail, axis, [(i, (i + 1) % count) for i in range(count)]),
                cells,
                lax.ppermute(head, axis, [((i + 1) % count, i) for i in range(count)]),
            ],
            axis=dim,
        )
    return cells


def apply_depth(block, z_factor):
    return lax.dot_general(
        block, z_factor, (((2,), (1,)), ((), ())), precision=lax.Precision.HIGHEST
    )


def apply_planes(x_panel, widened):
    return jnp.einsum("rj,yjz->yrz", x_panel, widened, precision=lax.Precision.HIGHEST)


def apply_across(block, y_factor):
    rows_here, planes, cells = block.shape
    flat = block.reshape(rows_here, planes * cells)
    pencils = lax.all_to_all(flat, "grp", split_axis=1, concat_axis=0, tiled=True)
    turned = jnp.dot(y_factor, pencils, precision=lax.Precision.HIGHEST)
    back = lax.all_to_all(turned, "grp", split_axis=0, concat_axis=1, tiled=True)
    return back.reshape(rows_here, planes, cells)


def plain(field, x_panel, y_factor, z_factor, scaling):
    width = (x_panel.shape[1] - field.shape[1]) // 2
    widened = padded(field, (("blk", 1),), width)
    planes_done = apply_planes(x_panel, widened)
    depth = apply_depth(planes_done, z_factor)
    along = apply_across(depth, y_factor)
    return along * scaling


def split(value):
    high = value.astype(BF16)
    return high, (value - high.astype(F32)).astype(BF16)


def stacked(value):
    high, low = split(value)
    return jnp.concatenate([high, low], axis=0), high


def times(both, high, right):
    right_high, right_low = split(right)
    rows = high.shape[0]
    first = jnp.dot(both, right_high, preferred_element_type=F32)
    second = jnp.dot(high, right_low, preferred_element_type=F32)
    return first[:rows] + (first[rows:] + second)


def kernel(
    n_grp, n_blk, field_in, panel_in, y_in, z_in, scaling_in, out,
    field, panel, y_factor, z_factor, scaling, done,
    field_high, field_low, own, partner, other, turned, gathered, mixed, back,
    in_sem, out_sem, f_send, f_recv, b_send, b_recv, h1_send, h1_recv, h2_send, h2_recv,
):
    rows, planes, cells = field.shape
    step_rows = rows // FETCHES
    row_parts = [pl.ds(i * step_rows, step_rows) for i in range(FETCHES)]
    grp = lax.axis_index("grp")
    blk = lax.axis_index("blk")
    half_grp, half_planes = n_grp // 2, planes // 2
    far = jnp.where(grp < half_grp, 1, 0)
    near = 1 - far
    starts = [pl.multiple_of(half * half_planes, SUB // 2) for half in (far, near)]
    heads = [pl.ds(0, LANES), pl.ds(LANES, cells - LANES)][: 1 + (cells > LANES)]
    sources = [(z_in.at[heads[0]], z_factor.at[heads[0]])]
    for start in starts:
        for at in row_parts:
            place = (at, pl.ds(start, half_planes))
            sources.append((field_in.at[place], field.at[place]))
    sources += [(z_in.at[at], z_factor.at[at]) for at in heads[1:]]
    sources += [(y_in, y_factor), (panel_in, panel), (scaling_in, scaling)]
    fetches = [pltpu.make_async_copy(*pair, in_sem.at[i]) for i, pair in enumerate(sources)]
    for fetch in fetches:
        fetch.start()
    chunks = cells // LANES
    share = planes // n_grp
    piece = share * rows
    parts = h1_send.shape[1]
    part_rows = rows // parts
    subs = f_send.shape[1]
    sub = share // subs
    sub_piece = sub * rows
    even = lax.rem(blk, 2) == 0
    mate = jnp.where(even, blk + 1, blk - 1)
    ahead = lax.rem(jnp.where(even, blk + 2, blk + n_blk - 2), n_blk)
    behind = lax.rem(jnp.where(even, blk + n_blk - 2, blk + 2), n_blk)

    far_ids = [far * half_grp + lax.rem(grp + k, half_grp) for k in range(half_grp)]
    near_ids = [near * half_grp + lax.rem(grp + k, half_grp) for k in range(1, half_grp)]
    barrier = pltpu.get_barrier_semaphore()
    for to in far_ids + near_ids:
        pl.semaphore_signal(barrier, inc=1, device_id={"grp": to}, device_id_type=MESH)
    pl.semaphore_signal(barrier, inc=1, device_id={"blk": mate}, device_id_type=MESH)
    pl.semaphore_signal(barrier, inc=1, device_id={"blk": behind}, device_id_type=MESH)

    def times_z(high, low, z_both, z_high):
        turn = (((1,), (1,)), ((), ()))
        first = lax.dot_general(high, z_both, turn, preferred_element_type=F32)
        second = lax.dot_general(low, z_high, turn, preferred_element_type=F32)
        return first[:, :LANES] + (first[:, LANES:] + second)

    def z_rows(chunk):
        return stacked(z_factor[chunk * LANES:(chunk + 1) * LANES, :])

    def first_depth(which, z_both, z_high):
        start = starts[which]
        for at in range(FETCHES):
            fetches[1 + which * FETCHES + at].wait()
            y = at * step_rows
            block = field[y:y + step_rows, pl.ds(start, half_planes), :]
            high, low = split(block.reshape(step_rows * half_planes, cells))
            result = times_z(high, low, z_both, z_high).reshape(step_rows, half_planes, LANES)
            for k in range(step_rows):
                turned[0, pl.ds(start * rows + y + k, half_planes, stride=rows), :] = result[k]

    def depth(chunk):
        z_both, z_high = z_rows(chunk)
        for y in range(0, rows, step_rows):
            y_end = y + step_rows
            here = slice(y * planes, y_end * planes)
            if chunk == 1:
                flat = field[y:y_end].reshape(step_rows * planes, cells)
                field_high[here, :], field_low[here, :] = split(flat)
            result = times_z(field_high[here, :], field_low[here, :], z_both, z_high)
            own[chunk, y:y_end] = result.reshape(step_rows, planes, LANES)

    def rows_of(y):
        return pl.ds(y, planes, stride=rows)

    def spot(device, at):
        return pl.ds(pl.multiple_of(device * piece + at * sub_piece, SUB), sub_piece)

    def scatter(chunk, ids):
        for at in range(subs):
            within = pl.ds(at * sub_piece, sub_piece)
            for to in ids:
                pltpu.make_async_remote_copy(
                    src_ref=turned.at[chunk, spot(to, at)],
                    dst_ref=gathered.at[chunk, grp, within],
                    send_sem=f_send.at[chunk, at],
                    recv_sem=f_recv.at[chunk, at],
                    device_id={"grp": to},
                    device_id_type=MESH,
                ).start()

    def keep(chunk):
        mine = pl.ds(pl.multiple_of(grp * piece, SUB), piece)
        gathered[chunk, grp] = turned[chunk, mine, :]

    def wait_for(ref, sem):
        pltpu.make_async_copy(ref, ref, sem).wait()

    def incoming(chunk):
        return gathered.at[chunk, pl.ds(0, n_grp - 1), pl.ds(0, sub_piece)]

    def across(chunk):
        y_both, y_high = stacked(y_factor[...])
        for at in range(subs):
            wait_for(incoming(chunk), f_recv.at[chunk, at])
            for plane in range(at * sub, (at + 1) * sub):
                here = slice(plane * rows, (plane + 1) * rows)
                pencils = jnp.concatenate(
                    [gathered[chunk, g, here, :] for g in range(n_grp)], axis=0
                )
                result = times(y_both, y_high, pencils)
                for g in range(n_grp):
                    mixed[chunk, g, here, :] = result[g * rows:(g + 1) * rows]
            within = pl.ds(at * sub_piece, sub_piece)
            for to in far_ids + near_ids:
                pltpu.make_async_remote_copy(
                    src_ref=mixed.at[chunk, to, within],
                    dst_ref=back.at[chunk, spot(grp, at)],
                    send_sem=b_send.at[chunk, at],
                    recv_sem=b_recv.at[chunk, at],
                    device_id={"grp": to},
                    device_id_type=MESH,
                ).start()
            back[chunk, spot(grp, at), :] = mixed[chunk, grp, at * sub_piece:(at + 1) * sub_piece, :]

    def wait_back(chunk):
        for at in range(subs):
            wait_for(back.at[chunk, pl.ds(0, (n_grp - 1) * sub_piece)], b_recv.at[chunk, at])

    def part(chunk, at):
        return (chunk, pl.ds(at * part_rows, part_rows))

    def swap(chunk, at):
        return pltpu.make_async_remote_copy(
            src_ref=own.at[part(chunk, at)],
            dst_ref=partner.at[part(chunk, at)],
            send_sem=h1_send.at[chunk, at],
            recv_sem=h1_recv.at[chunk, at],
            device_id={"blk": mate},
            device_id_type=MESH,
        )

    def forward(chunk, at):
        return pltpu.make_async_remote_copy(
            src_ref=partner.at[part(chunk, at)],
            dst_ref=other.at[part(chunk, at)],
            send_sem=h2_send.at[chunk, at],
            recv_sem=h2_recv.at[chunk, at],
            device_id={"blk": ahead},
            device_id_type=MESH,
        )

    def pass_on(chunk):
        for at in range(parts):
            swap(chunk, at).wait_recv()
            forward(chunk, at).start()

    def along(chunk, store):
        left, mid, right = (panel[:, i * planes:(i + 1) * planes] for i in range(3))
        factor = jnp.concatenate(
            [mid, jnp.where(even, right, left), jnp.where(even, left, right)], axis=1
        )
        x_both, x_high = stacked(factor)
        for at in range(parts):
            forward(chunk, at).wait_recv()
            for y in range(at * part_rows, (at + 1) * part_rows, 2):
                wide = jnp.concatenate(
                    [
                        jnp.concatenate([held[chunk, y + k] for held in (own, partner, other)], axis=0)
                        for k in range(2)
                    ],
                    axis=1,
                )
                result = times(x_both, x_high, wide)
                for k in range(2):
                    store(chunk, y + k, result[:, k * LANES:(k + 1) * LANES])

    def store_turned(chunk, y, value):
        turned[chunk, rows_of(y), :] = value

    def written(chunk, at):
        return pltpu.make_async_copy(
            done.at[chunk, row_parts[at]],
            out.at[row_parts[at], :, pl.ds(chunk * LANES, LANES)],
            out_sem.at[chunk, at],
        )

    def store_out(chunk, y, value):
        done[chunk, y] = value * scaling[y, :, chunk * LANES:(chunk + 1) * LANES]
        if (y + 1) % step_rows == 0:
            written(chunk, y // step_rows).start()

    fetches[0].wait()
    z_both, z_high = z_rows(0)
    first_depth(0, z_both, z_high)
    pl.semaphore_wait(barrier, n_grp + 1)
    scatter(0, far_ids)
    first_depth(1, z_both, z_high)
    scatter(0, near_ids)
    keep(0)
    for fetch in fetches[1 + 2 * FETCHES:]:
        fetch.wait()
    for chunk in range(1, chunks):
        depth(chunk)
        for at in range(parts):
            swap(chunk, at).start()

    def first_home():
        wait_back(0)
        for y in range(rows):
            own[0, y] = back[0, rows_of(y), :]
        for at in range(parts):
            swap(0, at).start()

    for chunk in range(1, chunks):
        pass_on(chunk)
        if chunk == 1:
            across(0)
        elif chunk == 2:
            first_home()
        else:
            across(chunk - 2)
        along(chunk, store_turned)
        scatter(chunk, far_ids + near_ids)
        keep(chunk)
    if chunks < 2:
        across(0)
    if chunks < 3:
        first_home()
    pass_on(0)
    late = range(max(1, chunks - 2), chunks)
    for chunk in late[:-1]:
        across(chunk)
    along(0, store_out)
    for chunk in late[-1:]:
        across(chunk)
    for chunk in range(1, chunks):
        wait_back(chunk)
        for y in range(rows):
            store_out(chunk, y, back[chunk, rows_of(y), :])
    for chunk in range(chunks):
        for at in range(FETCHES):
            written(chunk, at).wait()
        for at in range(subs):
            wait_for(incoming(chunk), f_send.at[chunk, at])
            wait_for(incoming(chunk), b_send.at[chunk, at])
        for at in range(parts):
            swap(chunk, at).wait_send()
            forward(chunk, at).wait_send()


def hand_on(source, target, sem):
    rows = source.shape[0]
    copies = [pltpu.make_async_copy(source.at[i], target.at[i], sem.at[i]) for i in range(rows)]
    for copy in copies:
        copy.start()
    for copy in copies:
        copy.wait()


def fused(field, x_panel, y_factor, z_factor, scaling):
    n_grp, n_blk = lax.axis_size("grp"), lax.axis_size("blk")
    rows, planes, cells = field.shape
    chunks = cells // LANES
    share = planes // n_grp
    piece = share * rows
    parts = 4
    subs = 2 if share % 2 == 0 else 1
    held = pltpu.VMEM((chunks, rows, planes, LANES), F32)
    turned = pltpu.VMEM((chunks, planes * rows, LANES), F32)
    pieces = pltpu.VMEM((chunks, n_grp, piece, LANES), F32)
    result = pl.pallas_call(
        functools.partial(kernel, n_grp, n_blk),
        out_shape=jax.ShapeDtypeStruct(field.shape, F32),
        in_specs=[pl.BlockSpec(memory_space=pltpu.HBM)] * 5,
        out_specs=pl.BlockSpec(memory_space=pltpu.HBM),
        scratch_shapes=[
            pltpu.VMEM(array.shape, F32) for array in (field, x_panel, y_factor, z_factor, scaling)
        ]
        + [held]
        + [pltpu.VMEM((rows * planes, cells), BF16)] * 2
        + [held] * 3
        + [turned, pieces, pieces, turned]
        + [pltpu.SemaphoreType.DMA((5 + 2 * FETCHES,))]
        + [pltpu.SemaphoreType.DMA((chunks, FETCHES))]
        + [pltpu.SemaphoreType.DMA((chunks, subs))] * 4
        + [pltpu.SemaphoreType.DMA((chunks, parts))] * 4,
        compiler_params=pltpu.CompilerParams(
            collective_id=0, has_side_effects=True, vmem_limit_bytes=60 * 2**20
        ),
    )(field, x_panel, y_factor, z_factor, scaling)
    return pl.pallas_call(
        hand_on,
        out_shape=jax.ShapeDtypeStruct(field.shape, F32),
        in_specs=[pl.BlockSpec(memory_space=pltpu.HBM)],
        out_specs=pl.BlockSpec(memory_space=pltpu.HBM),
        scratch_shapes=[pltpu.SemaphoreType.DMA((rows,))],
        compiler_params=pltpu.CompilerParams(vmem_limit_bytes=60 * 2**20),
    )(result)


def on_device(field, x_panel, y_factor, z_factor, scaling):
    n_grp, n_blk = lax.axis_size("grp"), lax.axis_size("blk")
    rows, planes, cells = field.shape
    fits = (
        x_panel.shape[1] == 3 * planes
        and n_blk >= 4
        and n_blk % 2 == 0
        and n_grp % 2 == 0
        and planes % n_grp == 0
        and planes % SUB == 0
        and rows % SUB == 0
        and cells % LANES == 0
    )
    step = fused if fits else plain
    return step(field, x_panel, y_factor, z_factor, scaling)


def solution(mesh):
    in_specs = (P("grp", "blk", None), P("blk", None), P(), P(), P("grp", "blk", None))
    out_specs = P("grp", "blk", None)
    return jax.shard_map(
        on_device, mesh=mesh, in_specs=in_specs, out_specs=out_specs, check_vma=False
    )
```

```python
import functools

import jax
import jax.numpy as jnp
from jax import lax
from jax.experimental import pallas as pl
from jax.experimental.pallas import tpu as pltpu
from jax.sharding import PartitionSpec as P

LANES = 128
SUB = 16
FETCHES = 4
MESH = pl.DeviceIdType.MESH
F32 = jnp.float32
BF16 = jnp.bfloat16


def padded(cells, sides, width):
    for axis, dim in sides:
        count = lax.axis_size(axis)
        head = lax.slice_in_dim(cells, 0, width, axis=dim)
        tail = lax.slice_in_dim(cells, cells.shape[dim] - width, cells.shape[dim], axis=dim)
        cells = jnp.concatenate(
            [
                lax.ppermute(tail, axis, [(i, (i + 1) % count) for i in range(count)]),
                cells,
                lax.ppermute(head, axis, [((i + 1) % count, i) for i in range(count)]),
            ],
            axis=dim,
        )
    return cells


def apply_depth(block, z_factor):
    return lax.dot_general(
        block, z_factor, (((2,), (1,)), ((), ())), precision=lax.Precision.HIGHEST
    )


def apply_planes(x_panel, widened):
    return jnp.einsum("rj,yjz->yrz", x_panel, widened, precision=lax.Precision.HIGHEST)


def apply_across(block, y_factor):
    rows_here, planes, cells = block.shape
    flat = block.reshape(rows_here, planes * cells)
    pencils = lax.all_to_all(flat, "grp", split_axis=1, concat_axis=0, tiled=True)
    turned = jnp.dot(y_factor, pencils, precision=lax.Precision.HIGHEST)
    back = lax.all_to_all(turned, "grp", split_axis=0, concat_axis=1, tiled=True)
    return back.reshape(rows_here, planes, cells)


def plain(field, x_panel, y_factor, z_factor, scaling):
    width = (x_panel.shape[1] - field.shape[1]) // 2
    widened = padded(field, (("blk", 1),), width)
    planes_done = apply_planes(x_panel, widened)
    depth = apply_depth(planes_done, z_factor)
    along = apply_across(depth, y_factor)
    return along * scaling


def split(value):
    high = value.astype(BF16)
    return high, (value - high.astype(F32)).astype(BF16)


def stacked(value):
    high, low = split(value)
    return jnp.concatenate([high, low], axis=0), high


def times(both, high, right):
    right_high, right_low = split(right)
    rows = high.shape[0]
    first = jnp.dot(both, right_high, preferred_element_type=F32)
    second = jnp.dot(high, right_low, preferred_element_type=F32)
    return first[:rows] + (first[rows:] + second)


def kernel(
    n_grp, n_blk, field_in, panel_in, y_in, z_in, scaling_in, out,
    field, panel, y_factor, z_factor, scaling,
    field_high, field_low, own, partner, other, turned, gathered, mixed, back,
    in_sem, f_send, f_recv, b_send, b_recv, h1_send, h1_recv, h2_send, h2_recv,
):
    rows, planes, cells = field.shape
    step_rows = rows // FETCHES
    row_parts = [pl.ds(i * step_rows, step_rows) for i in range(FETCHES)]
    heads = [pl.ds(0, LANES), pl.ds(LANES, cells - LANES)][: 1 + (cells > LANES)]
    sources = [(z_in.at[heads[0]], z_factor.at[heads[0]])]
    sources += [(field_in.at[at], field.at[at]) for at in row_parts]
    sources += [(z_in.at[at], z_factor.at[at]) for at in heads[1:]]
    sources += [(y_in, y_factor), (panel_in, panel), (scaling_in, scaling)]
    fetches = [pltpu.make_async_copy(*pair, in_sem.at[i]) for i, pair in enumerate(sources)]
    now, later = fetches[: 1 + FETCHES], fetches[1 + FETCHES:]
    for fetch in now:
        fetch.start()
    chunks = cells // LANES
    share = planes // n_grp
    piece = share * rows
    parts = h1_send.shape[1]
    part_rows = rows // parts
    subs = f_send.shape[1]
    sub = share // subs
    sub_piece = sub * rows
    grp = lax.axis_index("grp")
    blk = lax.axis_index("blk")
    even = lax.rem(blk, 2) == 0
    mate = jnp.where(even, blk + 1, blk - 1)
    ahead = lax.rem(jnp.where(even, blk + 2, blk + n_blk - 2), n_blk)
    behind = lax.rem(jnp.where(even, blk + n_blk - 2, blk + 2), n_blk)

    offsets = sorted(range(1, n_grp), key=lambda s: (-min(s, n_grp - s), s))
    barrier = pltpu.get_barrier_semaphore()
    for step in offsets:
        pl.semaphore_signal(
            barrier, inc=1, device_id={"grp": lax.rem(grp + step, n_grp)}, device_id_type=MESH
        )
    pl.semaphore_signal(barrier, inc=1, device_id={"blk": mate}, device_id_type=MESH)
    pl.semaphore_signal(barrier, inc=1, device_id={"blk": behind}, device_id_type=MESH)

    def depth(chunk):
        z_both, z_high = stacked(z_factor[chunk * LANES:(chunk + 1) * LANES, :])
        turn = (((1,), (1,)), ((), ()))
        for y in range(0, rows, step_rows):
            y_end = y + step_rows
            here = slice(y * planes, y_end * planes)
            if chunk == 0:
                fetches[1 + y // step_rows].wait()
                flat = field[y:y_end].reshape(step_rows * planes, cells)
                field_high[here, :], field_low[here, :] = split(flat)
            first = lax.dot_general(field_high[here, :], z_both, turn, preferred_element_type=F32)
            second = lax.dot_general(field_low[here, :], z_high, turn, preferred_element_type=F32)
            result = first[:, :LANES] + (first[:, LANES:] + second)
            result = result.reshape(step_rows, planes, LANES)
            if chunk == 0:
                for k in range(step_rows):
                    store_turned(chunk, y + k, result[k])
            else:
                own[chunk, y:y_end] = result

    def rows_of(y):
        return pl.ds(y, planes, stride=rows)

    def spot(device, at):
        return pl.ds(pl.multiple_of(device * piece + at * sub_piece, SUB), sub_piece)

    def scatter(chunk):
        for at in range(subs):
            within = pl.ds(at * sub_piece, sub_piece)
            for step in offsets:
                to = lax.rem(grp + step, n_grp)
                pltpu.make_async_remote_copy(
                    src_ref=turned.at[chunk, spot(to, at)],
                    dst_ref=gathered.at[chunk, grp, within],
                    send_sem=f_send.at[chunk, at],
                    recv_sem=f_recv.at[chunk, at],
                    device_id={"grp": to},
                    device_id_type=MESH,
                ).start()
        mine = pl.ds(pl.multiple_of(grp * piece, SUB), piece)
        gathered[chunk, grp] = turned[chunk, mine, :]

    def wait_for(ref, sem):
        pltpu.make_async_copy(ref, ref, sem).wait()

    def incoming(chunk):
        return gathered.at[chunk, pl.ds(0, n_grp - 1), pl.ds(0, sub_piece)]

    def across(chunk):
        y_both, y_high = stacked(y_factor[...])
        for at in range(subs):
            wait_for(incoming(chunk), f_recv.at[chunk, at])
            for plane in range(at * sub, (at + 1) * sub):
                here = slice(plane * rows, (plane + 1) * rows)
                pencils = jnp.concatenate(
                    [gathered[chunk, g, here, :] for g in range(n_grp)], axis=0
                )
                result = times(y_both, y_high, pencils)
                for g in range(n_grp):
                    mixed[chunk, g, here, :] = result[g * rows:(g + 1) * rows]
            within = pl.ds(at * sub_piece, sub_piece)
            for step in offsets:
                to = lax.rem(grp + step, n_grp)
                pltpu.make_async_remote_copy(
                    src_ref=mixed.at[chunk, to, within],
                    dst_ref=back.at[chunk, spot(grp, at)],
                    send_sem=b_send.at[chunk, at],
                    recv_sem=b_recv.at[chunk, at],
                    device_id={"grp": to},
                    device_id_type=MESH,
                ).start()
            back[chunk, spot(grp, at), :] = mixed[chunk, grp, at * sub_piece:(at + 1) * sub_piece, :]

    def wait_back(chunk):
        for at in range(subs):
            wait_for(back.at[chunk, pl.ds(0, (n_grp - 1) * sub_piece)], b_recv.at[chunk, at])

    def part(chunk, at):
        return (chunk, pl.ds(at * part_rows, part_rows))

    def swap(chunk, at):
        return pltpu.make_async_remote_copy(
            src_ref=own.at[part(chunk, at)],
            dst_ref=partner.at[part(chunk, at)],
            send_sem=h1_send.at[chunk, at],
            recv_sem=h1_recv.at[chunk, at],
            device_id={"blk": mate},
            device_id_type=MESH,
        )

    def forward(chunk, at):
        return pltpu.make_async_remote_copy(
            src_ref=partner.at[part(chunk, at)],
            dst_ref=other.at[part(chunk, at)],
            send_sem=h2_send.at[chunk, at],
            recv_sem=h2_recv.at[chunk, at],
            device_id={"blk": ahead},
            device_id_type=MESH,
        )

    def pass_on(chunk):
        for at in range(parts):
            swap(chunk, at).wait_recv()
            forward(chunk, at).start()

    def along(chunk, store):
        left, mid, right = (panel[:, i * planes:(i + 1) * planes] for i in range(3))
        factor = jnp.concatenate(
            [mid, jnp.where(even, right, left), jnp.where(even, left, right)], axis=1
        )
        x_both, x_high = stacked(factor)
        for at in range(parts):
            forward(chunk, at).wait_recv()
            for y in range(at * part_rows, (at + 1) * part_rows, 2):
                wide = jnp.concatenate(
                    [
                        jnp.concatenate([held[chunk, y + k] for held in (own, partner, other)], axis=0)
                        for k in range(2)
                    ],
                    axis=1,
                )
                result = times(x_both, x_high, wide)
                for k in range(2):
                    store(chunk, y + k, result[:, k * LANES:(k + 1) * LANES])

    def store_turned(chunk, y, value):
        turned[chunk, rows_of(y), :] = value

    def store_out(chunk, y, value):
        lanes = slice(chunk * LANES, (chunk + 1) * LANES)
        out[y, :, lanes] = value * scaling[y, :, lanes]

    fetches[0].wait()
    depth(0)
    for fetch in later:
        fetch.start()
    pl.semaphore_wait(barrier, len(offsets) + 2)
    scatter(0)
    for fetch in later:
        fetch.wait()
    for chunk in range(1, chunks):
        depth(chunk)
        for at in range(parts):
            swap(chunk, at).start()

    def first_home():
        wait_back(0)
        for y in range(rows):
            own[0, y] = back[0, rows_of(y), :]
        for at in range(parts):
            swap(0, at).start()

    for chunk in range(1, chunks):
        pass_on(chunk)
        if chunk == 1:
            across(0)
        elif chunk == 2:
            first_home()
        else:
            across(chunk - 2)
        along(chunk, store_turned)
        scatter(chunk)
    if chunks < 2:
        across(0)
    if chunks < 3:
        first_home()
    pass_on(0)
    late = range(max(1, chunks - 2), chunks)
    for chunk in late[:-1]:
        across(chunk)
    along(0, store_out)
    for chunk in late[-1:]:
        across(chunk)
    for chunk in range(chunks):
        for at in range(parts):
            swap(chunk, at).wait_send()
            forward(chunk, at).wait_send()
        for at in range(subs):
            wait_for(incoming(chunk), f_send.at[chunk, at])
    for chunk in range(1, chunks):
        wait_back(chunk)
        for y in range(rows):
            store_out(chunk, y, back[chunk, rows_of(y), :])
    for chunk in range(chunks):
        for at in range(subs):
            wait_for(incoming(chunk), b_send.at[chunk, at])


def fused(field, x_panel, y_factor, z_factor, scaling):
    n_grp, n_blk = lax.axis_size("grp"), lax.axis_size("blk")
    rows, planes, cells = field.shape
    chunks = cells // LANES
    share = planes // n_grp
    piece = share * rows
    parts = 4
    subs = 2 if share % 2 == 0 else 1
    held = pltpu.VMEM((chunks, rows, planes, LANES), F32)
    turned = pltpu.VMEM((chunks, planes * rows, LANES), F32)
    pieces = pltpu.VMEM((chunks, n_grp, piece, LANES), F32)
    return pl.pallas_call(
        functools.partial(kernel, n_grp, n_blk),
        out_shape=pltpu.VMEM(field.shape, F32),
        in_specs=[pl.BlockSpec(memory_space=pltpu.HBM)] * 5,
        out_specs=pl.BlockSpec(memory_space=pltpu.VMEM),
        scratch_shapes=[
            pltpu.VMEM(array.shape, F32) for array in (field, x_panel, y_factor, z_factor, scaling)
        ]
        + [pltpu.VMEM((rows * planes, cells), BF16)] * 2
        + [held] * 3
        + [turned, pieces, pieces, turned]
        + [pltpu.SemaphoreType.DMA((5 + FETCHES,))]
        + [pltpu.SemaphoreType.DMA((chunks, subs))] * 4
        + [pltpu.SemaphoreType.DMA((chunks, parts))] * 4,
        compiler_params=pltpu.CompilerParams(
            collective_id=0, has_side_effects=True, vmem_limit_bytes=40 * 2**20
        ),
    )(*(
        pltpu.with_memory_space_constraint(array, pltpu.HBM)
        for array in (field, x_panel, y_factor, z_factor, scaling)
    ))


def on_device(field, x_panel, y_factor, z_factor, scaling):
    n_grp, n_blk = lax.axis_size("grp"), lax.axis_size("blk")
    rows, planes, cells = field.shape
    fits = (
        x_panel.shape[1] == 3 * planes
        and n_blk >= 4
        and n_blk % 2 == 0
        and n_grp >= 2
        and planes % n_grp == 0
        and planes % SUB == 0
        and rows % SUB == 0
        and cells % LANES == 0
    )
    step = fused if fits else plain
    return step(field, x_panel, y_factor, z_factor, scaling)


def solution(mesh):
    in_specs = (P("grp", "blk", None), P("blk", None), P(), P(), P("grp", "blk", None))
    out_specs = P("grp", "blk", None)
    return jax.shard_map(
        on_device, mesh=mesh, in_specs=in_specs, out_specs=out_specs, check_vma=False
    )
```

```python
import functools

import jax
import jax.numpy as jnp
from jax import lax
from jax.experimental import pallas as pl
from jax.experimental.pallas import tpu as pltpu
from jax.sharding import PartitionSpec as P

LANES = 128
SUB = 16
FETCHES = 4
MESH = pl.DeviceIdType.MESH
F32 = jnp.float32
BF16 = jnp.bfloat16


def padded(cells, sides, width):
    for axis, dim in sides:
        count = lax.axis_size(axis)
        head = lax.slice_in_dim(cells, 0, width, axis=dim)
        tail = lax.slice_in_dim(cells, cells.shape[dim] - width, cells.shape[dim], axis=dim)
        cells = jnp.concatenate(
            [
                lax.ppermute(tail, axis, [(i, (i + 1) % count) for i in range(count)]),
                cells,
                lax.ppermute(head, axis, [((i + 1) % count, i) for i in range(count)]),
            ],
            axis=dim,
        )
    return cells


def apply_depth(block, z_factor):
    return lax.dot_general(
        block, z_factor, (((2,), (1,)), ((), ())), precision=lax.Precision.HIGHEST
    )


def apply_planes(x_panel, widened):
    return jnp.einsum("rj,yjz->yrz", x_panel, widened, precision=lax.Precision.HIGHEST)


def apply_across(block, y_factor):
    rows_here, planes, cells = block.shape
    flat = block.reshape(rows_here, planes * cells)
    pencils = lax.all_to_all(flat, "grp", split_axis=1, concat_axis=0, tiled=True)
    turned = jnp.dot(y_factor, pencils, precision=lax.Precision.HIGHEST)
    back = lax.all_to_all(turned, "grp", split_axis=0, concat_axis=1, tiled=True)
    return back.reshape(rows_here, planes, cells)


def plain(field, x_panel, y_factor, z_factor, scaling):
    width = (x_panel.shape[1] - field.shape[1]) // 2
    widened = padded(field, (("blk", 1),), width)
    planes_done = apply_planes(x_panel, widened)
    depth = apply_depth(planes_done, z_factor)
    along = apply_across(depth, y_factor)
    return along * scaling


def split(value):
    high = value.astype(BF16)
    return high, (value - high.astype(F32)).astype(BF16)


def stacked(value):
    high, low = split(value)
    return jnp.concatenate([high, low], axis=0), high


def times(both, high, right):
    right_high, right_low = split(right)
    rows = high.shape[0]
    first = jnp.dot(both, right_high, preferred_element_type=F32)
    second = jnp.dot(high, right_low, preferred_element_type=F32)
    return first[:rows] + (first[rows:] + second)


def kernel(
    n_grp, n_blk, field_in, panel_in, y_in, z_in, scaling_in, out,
    field, panel, y_factor, z_factor, scaling,
    field_high, field_low, own, partner, other, turned, gathered, mixed, back,
    in_sem, f_send, f_recv, b_send, b_recv, h1_send, h1_recv, h2_send, h2_recv,
):
    rows, planes, cells = field.shape
    step_rows = rows // FETCHES
    row_parts = [pl.ds(i * step_rows, step_rows) for i in range(FETCHES)]
    grp = lax.axis_index("grp")
    blk = lax.axis_index("blk")
    half_grp, half_planes = n_grp // 2, planes // 2
    far = jnp.where(grp < half_grp, 1, 0)
    near = 1 - far
    starts = [pl.multiple_of(half * half_planes, SUB // 2) for half in (far, near)]
    heads = [pl.ds(0, LANES), pl.ds(LANES, cells - LANES)][: 1 + (cells > LANES)]
    sources = [(z_in.at[heads[0]], z_factor.at[heads[0]])]
    for start in starts:
        for at in row_parts:
            place = (at, pl.ds(start, half_planes))
            sources.append((field_in.at[place], field.at[place]))
    sources += [(z_in.at[at], z_factor.at[at]) for at in heads[1:]]
    sources += [(y_in, y_factor), (panel_in, panel), (scaling_in, scaling)]
    fetches = [pltpu.make_async_copy(*pair, in_sem.at[i]) for i, pair in enumerate(sources)]
    now, later = fetches[: 1 + 2 * FETCHES], fetches[1 + 2 * FETCHES:]
    for fetch in now:
        fetch.start()
    chunks = cells // LANES
    share = planes // n_grp
    piece = share * rows
    parts = h1_send.shape[1]
    part_rows = rows // parts
    subs = f_send.shape[1]
    sub = share // subs
    sub_piece = sub * rows
    even = lax.rem(blk, 2) == 0
    mate = jnp.where(even, blk + 1, blk - 1)
    ahead = lax.rem(jnp.where(even, blk + 2, blk + n_blk - 2), n_blk)
    behind = lax.rem(jnp.where(even, blk + n_blk - 2, blk + 2), n_blk)

    far_ids = [far * half_grp + lax.rem(grp + k, half_grp) for k in range(half_grp)]
    near_ids = [near * half_grp + lax.rem(grp + k, half_grp) for k in range(1, half_grp)]
    offsets = sorted(range(1, n_grp), key=lambda s: (-min(s, n_grp - s), s))
    mixed_ids = [lax.rem(grp + step, n_grp) for step in offsets]
    barrier = pltpu.get_barrier_semaphore()
    for to in mixed_ids:
        pl.semaphore_signal(barrier, inc=1, device_id={"grp": to}, device_id_type=MESH)
    pl.semaphore_signal(barrier, inc=1, device_id={"blk": mate}, device_id_type=MESH)
    pl.semaphore_signal(barrier, inc=1, device_id={"blk": behind}, device_id_type=MESH)

    def times_z(high, low, z_both, z_high):
        turn = (((1,), (1,)), ((), ()))
        first = lax.dot_general(high, z_both, turn, preferred_element_type=F32)
        second = lax.dot_general(low, z_high, turn, preferred_element_type=F32)
        return first[:, :LANES] + (first[:, LANES:] + second)

    def z_rows(chunk):
        return stacked(z_factor[chunk * LANES:(chunk + 1) * LANES, :])

    def first_depth(which, z_both, z_high):
        start = starts[which]
        for at in range(FETCHES):
            fetches[1 + which * FETCHES + at].wait()
            y = at * step_rows
            block = field[y:y + step_rows, pl.ds(start, half_planes), :]
            high, low = split(block.reshape(step_rows * half_planes, cells))
            result = times_z(high, low, z_both, z_high).reshape(step_rows, half_planes, LANES)
            for k in range(step_rows):
                turned[0, pl.ds(start * rows + y + k, half_planes, stride=rows), :] = result[k]

    def depth(chunk):
        z_both, z_high = z_rows(chunk)
        for y in range(0, rows, step_rows):
            y_end = y + step_rows
            here = slice(y * planes, y_end * planes)
            if chunk == 1:
                flat = field[y:y_end].reshape(step_rows * planes, cells)
                field_high[here, :], field_low[here, :] = split(flat)
            result = times_z(field_high[here, :], field_low[here, :], z_both, z_high)
            own[chunk, y:y_end] = result.reshape(step_rows, planes, LANES)

    def rows_of(y):
        return pl.ds(y, planes, stride=rows)

    def spot(device, at):
        return pl.ds(pl.multiple_of(device * piece + at * sub_piece, SUB), sub_piece)

    def scatter(chunk, ids):
        for at in range(subs):
            within = pl.ds(at * sub_piece, sub_piece)
            for to in ids:
                pltpu.make_async_remote_copy(
                    src_ref=turned.at[chunk, spot(to, at)],
                    dst_ref=gathered.at[chunk, grp, within],
                    send_sem=f_send.at[chunk, at],
                    recv_sem=f_recv.at[chunk, at],
                    device_id={"grp": to},
                    device_id_type=MESH,
                ).start()

    def keep(chunk):
        mine = pl.ds(pl.multiple_of(grp * piece, SUB), piece)
        gathered[chunk, grp] = turned[chunk, mine, :]

    def wait_for(ref, sem):
        pltpu.make_async_copy(ref, ref, sem).wait()

    def incoming(chunk):
        return gathered.at[chunk, pl.ds(0, n_grp - 1), pl.ds(0, sub_piece)]

    def across(chunk):
        y_both, y_high = stacked(y_factor[...])
        for at in range(subs):
            wait_for(incoming(chunk), f_recv.at[chunk, at])
            for plane in range(at * sub, (at + 1) * sub):
                here = slice(plane * rows, (plane + 1) * rows)
                pencils = jnp.concatenate(
                    [gathered[chunk, g, here, :] for g in range(n_grp)], axis=0
                )
                result = times(y_both, y_high, pencils)
                for g in range(n_grp):
                    mixed[chunk, g, here, :] = result[g * rows:(g + 1) * rows]
            within = pl.ds(at * sub_piece, sub_piece)
            for to in mixed_ids:
                pltpu.make_async_remote_copy(
                    src_ref=mixed.at[chunk, to, within],
                    dst_ref=back.at[chunk, spot(grp, at)],
                    send_sem=b_send.at[chunk, at],
                    recv_sem=b_recv.at[chunk, at],
                    device_id={"grp": to},
                    device_id_type=MESH,
                ).start()
            back[chunk, spot(grp, at), :] = mixed[chunk, grp, at * sub_piece:(at + 1) * sub_piece, :]

    def wait_back(chunk):
        for at in range(subs):
            wait_for(back.at[chunk, pl.ds(0, (n_grp - 1) * sub_piece)], b_recv.at[chunk, at])

    def part(chunk, at):
        return (chunk, pl.ds(at * part_rows, part_rows))

    def swap(chunk, at):
        return pltpu.make_async_remote_copy(
            src_ref=own.at[part(chunk, at)],
            dst_ref=partner.at[part(chunk, at)],
            send_sem=h1_send.at[chunk, at],
            recv_sem=h1_recv.at[chunk, at],
            device_id={"blk": mate},
            device_id_type=MESH,
        )

    def forward(chunk, at):
        return pltpu.make_async_remote_copy(
            src_ref=partner.at[part(chunk, at)],
            dst_ref=other.at[part(chunk, at)],
            send_sem=h2_send.at[chunk, at],
            recv_sem=h2_recv.at[chunk, at],
            device_id={"blk": ahead},
            device_id_type=MESH,
        )

    def pass_on(chunk):
        for at in range(parts):
            swap(chunk, at).wait_recv()
            forward(chunk, at).start()

    def along(chunk, store):
        left, mid, right = (panel[:, i * planes:(i + 1) * planes] for i in range(3))
        factor = jnp.concatenate(
            [mid, jnp.where(even, right, left), jnp.where(even, left, right)], axis=1
        )
        x_both, x_high = stacked(factor)
        for at in range(parts):
            forward(chunk, at).wait_recv()
            for y in range(at * part_rows, (at + 1) * part_rows, 2):
                wide = jnp.concatenate(
                    [
                        jnp.concatenate([held[chunk, y + k] for held in (own, partner, other)], axis=0)
                        for k in range(2)
                    ],
                    axis=1,
                )
                result = times(x_both, x_high, wide)
                for k in range(2):
                    store(chunk, y + k, result[:, k * LANES:(k + 1) * LANES])

    def store_turned(chunk, y, value):
        turned[chunk, rows_of(y), :] = value

    def store_out(chunk, y, value):
        lanes = slice(chunk * LANES, (chunk + 1) * LANES)
        out[y, :, lanes] = value * scaling[y, :, lanes]

    fetches[0].wait()
    z_both, z_high = z_rows(0)
    first_depth(0, z_both, z_high)
    pl.semaphore_wait(barrier, len(offsets) + 2)
    scatter(0, far_ids)
    for fetch in later:
        fetch.start()
    first_depth(1, z_both, z_high)
    scatter(0, near_ids)
    keep(0)
    for fetch in later:
        fetch.wait()
    for chunk in range(1, chunks):
        depth(chunk)
        for at in range(parts):
            swap(chunk, at).start()

    def first_home():
        wait_back(0)
        for y in range(rows):
            own[0, y] = back[0, rows_of(y), :]
        for at in range(parts):
            swap(0, at).start()

    for chunk in range(1, chunks):
        pass_on(chunk)
        if chunk == 1:
            across(0)
        elif chunk == 2:
            first_home()
        else:
            across(chunk - 2)
        along(chunk, store_turned)
        scatter(chunk, mixed_ids)
        keep(chunk)
    if chunks < 2:
        across(0)
    if chunks < 3:
        first_home()
    pass_on(0)
    late = range(max(1, chunks - 2), chunks)
    for chunk in late[:-1]:
        across(chunk)
    along(0, store_out)
    for chunk in late[-1:]:
        across(chunk)
    for chunk in range(chunks):
        for at in range(parts):
            swap(chunk, at).wait_send()
            forward(chunk, at).wait_send()
        for at in range(subs):
            wait_for(incoming(chunk), f_send.at[chunk, at])
    for chunk in range(1, chunks):
        wait_back(chunk)
        for y in range(rows):
            store_out(chunk, y, back[chunk, rows_of(y), :])
    for chunk in range(chunks):
        for at in range(subs):
            wait_for(incoming(chunk), b_send.at[chunk, at])


def fused(field, x_panel, y_factor, z_factor, scaling):
    n_grp, n_blk = lax.axis_size("grp"), lax.axis_size("blk")
    rows, planes, cells = field.shape
    chunks = cells // LANES
    share = planes // n_grp
    piece = share * rows
    parts = 4
    subs = 2 if share % 2 == 0 else 1
    held = pltpu.VMEM((chunks, rows, planes, LANES), F32)
    turned = pltpu.VMEM((chunks, planes * rows, LANES), F32)
    pieces = pltpu.VMEM((chunks, n_grp, piece, LANES), F32)
    return pl.pallas_call(
        functools.partial(kernel, n_grp, n_blk),
        out_shape=pltpu.VMEM(field.shape, F32),
        in_specs=[pl.BlockSpec(memory_space=pltpu.HBM)] * 5,
        out_specs=pl.BlockSpec(memory_space=pltpu.VMEM),
        scratch_shapes=[
            pltpu.VMEM(array.shape, F32) for array in (field, x_panel, y_factor, z_factor, scaling)
        ]
        + [pltpu.VMEM((rows * planes, cells), BF16)] * 2
        + [held] * 3
        + [turned, pieces, pieces, turned]
        + [pltpu.SemaphoreType.DMA((5 + 2 * FETCHES,))]
        + [pltpu.SemaphoreType.DMA((chunks, subs))] * 4
        + [pltpu.SemaphoreType.DMA((chunks, parts))] * 4,
        compiler_params=pltpu.CompilerParams(
            collective_id=0, has_side_effects=True, vmem_limit_bytes=40 * 2**20
        ),
    )(*(
        pltpu.with_memory_space_constraint(array, pltpu.HBM)
        for array in (field, x_panel, y_factor, z_factor, scaling)
    ))


def on_device(field, x_panel, y_factor, z_factor, scaling):
    n_grp, n_blk = lax.axis_size("grp"), lax.axis_size("blk")
    rows, planes, cells = field.shape
    fits = (
        x_panel.shape[1] == 3 * planes
        and n_blk >= 4
        and n_blk % 2 == 0
        and n_grp % 2 == 0
        and planes % n_grp == 0
        and planes % SUB == 0
        and rows % SUB == 0
        and cells % LANES == 0
    )
    step = fused if fits else plain
    return step(field, x_panel, y_factor, z_factor, scaling)


def solution(mesh):
    in_specs = (P("grp", "blk", None), P("blk", None), P(), P(), P("grp", "blk", None))
    out_specs = P("grp", "blk", None)
    return jax.shard_map(
        on_device, mesh=mesh, in_specs=in_specs, out_specs=out_specs, check_vma=False
    )
```

```python
import functools

import jax
import jax.numpy as jnp
from jax import lax
from jax.experimental import pallas as pl
from jax.experimental.pallas import tpu as pltpu
from jax.sharding import PartitionSpec as P

LANES = 128
SUB = 16
FETCHES = 4
MESH = pl.DeviceIdType.MESH
F32 = jnp.float32
BF16 = jnp.bfloat16


def padded(cells, sides, width):
    for axis, dim in sides:
        count = lax.axis_size(axis)
        head = lax.slice_in_dim(cells, 0, width, axis=dim)
        tail = lax.slice_in_dim(cells, cells.shape[dim] - width, cells.shape[dim], axis=dim)
        cells = jnp.concatenate(
            [
                lax.ppermute(tail, axis, [(i, (i + 1) % count) for i in range(count)]),
                cells,
                lax.ppermute(head, axis, [((i + 1) % count, i) for i in range(count)]),
            ],
            axis=dim,
        )
    return cells


def apply_depth(block, z_factor):
    return lax.dot_general(
        block, z_factor, (((2,), (1,)), ((), ())), precision=lax.Precision.HIGHEST
    )


def apply_planes(x_panel, widened):
    return jnp.einsum("rj,yjz->yrz", x_panel, widened, precision=lax.Precision.HIGHEST)


def apply_across(block, y_factor):
    rows_here, planes, cells = block.shape
    flat = block.reshape(rows_here, planes * cells)
    pencils = lax.all_to_all(flat, "grp", split_axis=1, concat_axis=0, tiled=True)
    turned = jnp.dot(y_factor, pencils, precision=lax.Precision.HIGHEST)
    back = lax.all_to_all(turned, "grp", split_axis=0, concat_axis=1, tiled=True)
    return back.reshape(rows_here, planes, cells)


def plain(field, x_panel, y_factor, z_factor, scaling):
    width = (x_panel.shape[1] - field.shape[1]) // 2
    widened = padded(field, (("blk", 1),), width)
    planes_done = apply_planes(x_panel, widened)
    depth = apply_depth(planes_done, z_factor)
    along = apply_across(depth, y_factor)
    return along * scaling


def split(value):
    high = value.astype(BF16)
    return high, (value - high.astype(F32)).astype(BF16)


def stacked(value):
    high, low = split(value)
    return jnp.concatenate([high, low], axis=0), high


def times(both, high, right):
    right_high, right_low = split(right)
    rows = high.shape[0]
    first = jnp.dot(both, right_high, preferred_element_type=F32)
    second = jnp.dot(high, right_low, preferred_element_type=F32)
    return first[:rows] + (first[rows:] + second)


def kernel(
    n_grp, n_blk, field_in, panel_in, y_in, z_in, scaling_in, out,
    field, panel, y_factor, z_factor, scaling,
    field_high, field_low, own, partner, other, turned, gathered, mixed, back,
    in_sem, f_send, f_recv, b_send, b_recv, h1_send, h1_recv, h2_send, h2_recv,
):
    rows, planes, cells = field.shape
    step_rows = rows // FETCHES
    row_parts = [pl.ds(i * step_rows, step_rows) for i in range(FETCHES)]
    grp = lax.axis_index("grp")
    blk = lax.axis_index("blk")
    half_grp, half_planes = n_grp // 2, planes // 2
    far = jnp.where(grp < half_grp, 1, 0)
    near = 1 - far
    starts = [pl.multiple_of(half * half_planes, SUB // 2) for half in (far, near)]
    heads = [pl.ds(0, LANES), pl.ds(LANES, cells - LANES)][: 1 + (cells > LANES)]
    sources = [(z_in.at[heads[0]], z_factor.at[heads[0]])]
    for start in starts:
        for at in row_parts:
            place = (at, pl.ds(start, half_planes))
            sources.append((field_in.at[place], field.at[place]))
    sources += [(z_in.at[at], z_factor.at[at]) for at in heads[1:]]
    sources += [(y_in, y_factor), (panel_in, panel), (scaling_in, scaling)]
    fetches = [pltpu.make_async_copy(*pair, in_sem.at[i]) for i, pair in enumerate(sources)]
    now, later = fetches[: 1 + 2 * FETCHES], fetches[1 + 2 * FETCHES:]
    for fetch in now:
        fetch.start()
    chunks = cells // LANES
    share = planes // n_grp
    piece = share * rows
    parts = h1_send.shape[1]
    part_rows = rows // parts
    subs = f_send.shape[1]
    sub = share // subs
    sub_piece = sub * rows
    even = lax.rem(blk, 2) == 0
    mate = jnp.where(even, blk + 1, blk - 1)
    ahead = lax.rem(jnp.where(even, blk + 2, blk + n_blk - 2), n_blk)
    behind = lax.rem(jnp.where(even, blk + n_blk - 2, blk + 2), n_blk)

    far_ids = [far * half_grp + lax.rem(grp + k, half_grp) for k in range(half_grp)]
    near_ids = [near * half_grp + lax.rem(grp + k, half_grp) for k in range(1, half_grp)]
    offsets = sorted(range(1, n_grp), key=lambda s: (-min(s, n_grp - s), s))
    mixed_ids = [lax.rem(grp + step, n_grp) for step in offsets]
    barrier = pltpu.get_barrier_semaphore()
    for to in mixed_ids:
        pl.semaphore_signal(barrier, inc=1, device_id={"grp": to}, device_id_type=MESH)
    pl.semaphore_signal(barrier, inc=1, device_id={"blk": mate}, device_id_type=MESH)
    pl.semaphore_signal(barrier, inc=1, device_id={"blk": behind}, device_id_type=MESH)

    def times_z(high, low, z_both, z_high):
        turn = (((1,), (1,)), ((), ()))
        first = lax.dot_general(high, z_both, turn, preferred_element_type=F32)
        second = lax.dot_general(low, z_high, turn, preferred_element_type=F32)
        return first[:, :LANES] + (first[:, LANES:] + second)

    def z_rows(chunk):
        return stacked(z_factor[chunk * LANES:(chunk + 1) * LANES, :])

    def first_depth(which, z_both, z_high):
        start = starts[which]
        for at in range(FETCHES):
            fetches[1 + which * FETCHES + at].wait()
            y = at * step_rows
            block = field[y:y + step_rows, pl.ds(start, half_planes), :]
            high, low = split(block.reshape(step_rows * half_planes, cells))
            result = times_z(high, low, z_both, z_high).reshape(step_rows, half_planes, LANES)
            for k in range(step_rows):
                turned[0, pl.ds(start * rows + y + k, half_planes, stride=rows), :] = result[k]

    def depth(chunk):
        z_both, z_high = z_rows(chunk)
        for y in range(0, rows, step_rows):
            y_end = y + step_rows
            here = slice(y * planes, y_end * planes)
            if chunk == 1:
                flat = field[y:y_end].reshape(step_rows * planes, cells)
                field_high[here, :], field_low[here, :] = split(flat)
            result = times_z(field_high[here, :], field_low[here, :], z_both, z_high)
            own[chunk, y:y_end] = result.reshape(step_rows, planes, LANES)

    def rows_of(y):
        return pl.ds(y, planes, stride=rows)

    def spot(device, at):
        return pl.ds(pl.multiple_of(device * piece + at * sub_piece, SUB), sub_piece)

    def scatter(chunk, ids):
        for at in range(subs):
            within = pl.ds(at * sub_piece, sub_piece)
            for to in ids:
                pltpu.make_async_remote_copy(
                    src_ref=turned.at[chunk, spot(to, at)],
                    dst_ref=gathered.at[chunk, grp, within],
                    send_sem=f_send.at[chunk, at],
                    recv_sem=f_recv.at[chunk, at],
                    device_id={"grp": to},
                    device_id_type=MESH,
                ).start()

    def keep(chunk):
        mine = pl.ds(pl.multiple_of(grp * piece, SUB), piece)
        gathered[chunk, grp] = turned[chunk, mine, :]

    def wait_for(ref, sem):
        pltpu.make_async_copy(ref, ref, sem).wait()

    def incoming(chunk):
        return gathered.at[chunk, pl.ds(0, n_grp - 1), pl.ds(0, sub_piece)]

    def across_part(chunk, at):
        y_both, y_high = stacked(y_factor[...])
        wait_for(incoming(chunk), f_recv.at[chunk, at])
        for plane in range(at * sub, (at + 1) * sub):
            here = slice(plane * rows, (plane + 1) * rows)
            pencils = jnp.concatenate(
                [gathered[chunk, g, here, :] for g in range(n_grp)], axis=0
            )
            result = times(y_both, y_high, pencils)
            for g in range(n_grp):
                mixed[chunk, g, here, :] = result[g * rows:(g + 1) * rows]
        within = pl.ds(at * sub_piece, sub_piece)
        for to in mixed_ids:
            pltpu.make_async_remote_copy(
                src_ref=mixed.at[chunk, to, within],
                dst_ref=back.at[chunk, spot(grp, at)],
                send_sem=b_send.at[chunk, at],
                recv_sem=b_recv.at[chunk, at],
                device_id={"grp": to},
                device_id_type=MESH,
            ).start()
        back[chunk, spot(grp, at), :] = mixed[chunk, grp, at * sub_piece:(at + 1) * sub_piece, :]

    def across(chunk):
        for at in range(subs):
            across_part(chunk, at)

    def wait_back(chunk):
        for at in range(subs):
            wait_for(back.at[chunk, pl.ds(0, (n_grp - 1) * sub_piece)], b_recv.at[chunk, at])

    def part(chunk, at):
        return (chunk, pl.ds(at * part_rows, part_rows))

    def swap(chunk, at):
        return pltpu.make_async_remote_copy(
            src_ref=own.at[part(chunk, at)],
            dst_ref=partner.at[part(chunk, at)],
            send_sem=h1_send.at[chunk, at],
            recv_sem=h1_recv.at[chunk, at],
            device_id={"blk": mate},
            device_id_type=MESH,
        )

    def forward(chunk, at):
        return pltpu.make_async_remote_copy(
            src_ref=partner.at[part(chunk, at)],
            dst_ref=other.at[part(chunk, at)],
            send_sem=h2_send.at[chunk, at],
            recv_sem=h2_recv.at[chunk, at],
            device_id={"blk": ahead},
            device_id_type=MESH,
        )

    def pass_part(chunk, at):
        swap(chunk, at).wait_recv()
        forward(chunk, at).start()

    def pass_on(chunk):
        for at in range(parts):
            pass_part(chunk, at)

    def along(chunk, store):
        left, mid, right = (panel[:, i * planes:(i + 1) * planes] for i in range(3))
        factor = jnp.concatenate(
            [mid, jnp.where(even, right, left), jnp.where(even, left, right)], axis=1
        )
        x_both, x_high = stacked(factor)
        for at in range(parts):
            forward(chunk, at).wait_recv()
            for y in range(at * part_rows, (at + 1) * part_rows, 2):
                wide = jnp.concatenate(
                    [
                        jnp.concatenate([held[chunk, y + k] for held in (own, partner, other)], axis=0)
                        for k in range(2)
                    ],
                    axis=1,
                )
                result = times(x_both, x_high, wide)
                for k in range(2):
                    store(chunk, y + k, result[:, k * LANES:(k + 1) * LANES])

    def store_turned(chunk, y, value):
        turned[chunk, rows_of(y), :] = value

    def store_out(chunk, y, value):
        lanes = slice(chunk * LANES, (chunk + 1) * LANES)
        out[y, :, lanes] = value * scaling[y, :, lanes]

    fetches[0].wait()
    z_both, z_high = z_rows(0)
    first_depth(0, z_both, z_high)
    pl.semaphore_wait(barrier, len(offsets) + 2)
    scatter(0, far_ids)
    for fetch in later:
        fetch.start()
    first_depth(1, z_both, z_high)
    scatter(0, near_ids)
    keep(0)
    for fetch in later:
        fetch.wait()
    for chunk in range(1, chunks):
        depth(chunk)
        for at in range(parts):
            swap(chunk, at).start()

    def first_home():
        wait_back(0)
        for y in range(rows):
            own[0, y] = back[0, rows_of(y), :]
        for at in range(parts):
            swap(0, at).start()

    for chunk in range(1, chunks):
        if chunk == 1:
            for at in range(parts):
                pass_part(chunk, at)
                if at % (parts // subs) == 0:
                    across_part(0, at // (parts // subs))
        elif chunk == 2:
            pass_on(chunk)
            first_home()
        else:
            pass_on(chunk)
            across(chunk - 2)
        along(chunk, store_turned)
        scatter(chunk, mixed_ids)
        keep(chunk)
    if chunks < 2:
        across(0)
    if chunks < 3:
        first_home()
    pass_on(0)
    late = range(max(1, chunks - 2), chunks)
    for chunk in late[:-1]:
        across(chunk)
    along(0, store_out)
    for chunk in late[-1:]:
        across(chunk)
    for chunk in range(chunks):
        for at in range(parts):
            swap(chunk, at).wait_send()
            forward(chunk, at).wait_send()
        for at in range(subs):
            wait_for(incoming(chunk), f_send.at[chunk, at])
    for chunk in range(1, chunks):
        wait_back(chunk)
        for y in range(rows):
            store_out(chunk, y, back[chunk, rows_of(y), :])
    for chunk in range(chunks):
        for at in range(subs):
            wait_for(incoming(chunk), b_send.at[chunk, at])


def fused(field, x_panel, y_factor, z_factor, scaling):
    n_grp, n_blk = lax.axis_size("grp"), lax.axis_size("blk")
    rows, planes, cells = field.shape
    chunks = cells // LANES
    share = planes // n_grp
    piece = share * rows
    parts = 4
    subs = 2 if share % 2 == 0 else 1
    held = pltpu.VMEM((chunks, rows, planes, LANES), F32)
    turned = pltpu.VMEM((chunks, planes * rows, LANES), F32)
    pieces = pltpu.VMEM((chunks, n_grp, piece, LANES), F32)
    return pl.pallas_call(
        functools.partial(kernel, n_grp, n_blk),
        out_shape=pltpu.VMEM(field.shape, F32),
        in_specs=[pl.BlockSpec(memory_space=pltpu.HBM)] * 5,
        out_specs=pl.BlockSpec(memory_space=pltpu.VMEM),
        scratch_shapes=[
            pltpu.VMEM(array.shape, F32) for array in (field, x_panel, y_factor, z_factor, scaling)
        ]
        + [pltpu.VMEM((rows * planes, cells), BF16)] * 2
        + [held] * 3
        + [turned, pieces, pieces, turned]
        + [pltpu.SemaphoreType.DMA((5 + 2 * FETCHES,))]
        + [pltpu.SemaphoreType.DMA((chunks, subs))] * 4
        + [pltpu.SemaphoreType.DMA((chunks, parts))] * 4,
        compiler_params=pltpu.CompilerParams(
            collective_id=0, has_side_effects=True, vmem_limit_bytes=40 * 2**20
        ),
    )(*(
        pltpu.with_memory_space_constraint(array, pltpu.HBM)
        for array in (field, x_panel, y_factor, z_factor, scaling)
    ))


def on_device(field, x_panel, y_factor, z_factor, scaling):
    n_grp, n_blk = lax.axis_size("grp"), lax.axis_size("blk")
    rows, planes, cells = field.shape
    fits = (
        x_panel.shape[1] == 3 * planes
        and n_blk >= 4
        and n_blk % 2 == 0
        and n_grp % 2 == 0
        and planes % n_grp == 0
        and planes % SUB == 0
        and rows % SUB == 0
        and cells % LANES == 0
    )
    step = fused if fits else plain
    return step(field, x_panel, y_factor, z_factor, scaling)


def solution(mesh):
    in_specs = (P("grp", "blk", None), P("blk", None), P(), P(), P("grp", "blk", None))
    out_specs = P("grp", "blk", None)
    return jax.shard_map(
        on_device, mesh=mesh, in_specs=in_specs, out_specs=out_specs, check_vma=False
    )
```
